128 devices in a mesh: wide: 32 (over y, z, x_hi), narrow: 4 (over x_lo, core).
Axes of the slice: x: 4 (x_hi: 2, x_lo: 2; x = x_hi * 2 + x_lo), y: 4, z: 4, core: 2. Of those that a mesh axis runs over, the one named last changes fastest.
Arguments:
- hidden_in: bfloat16 [2, 8192, 768], P(None, ('wide', 'narrow')), may hold values from -6 to 6
- lengths: int32 [2], replicated, may hold values from 2048 to 8192, as said below
- w_qkv: bfloat16 [768, 2304], P('wide', 'narrow'), may hold values from -0.3125 to 0.3125
- w_out: bfloat16 [768, 768], P('wide', 'narrow'), may hold values from -1.75 to 1.75
- w_gate: bfloat16 [768, 3072], P('wide', 'narrow'), may hold values from -0.21875 to 0.21875
- w_up: bfloat16 [768, 3072], P('wide', 'narrow'), may hold values from -0.21875 to 0.21875
- w_down: bfloat16 [3072, 768], P('wide', 'narrow'), may hold values from -0.21875 to 0.21875
- norm_params: bfloat16 [4, 768], P('narrow', 'wide'), may hold values from 0.5 to 1.5
- cotangent: bfloat16 [2, 8192, 768], P(None, ('wide', 'narrow')), may hold values from -6 to 6
Outputs:
- layer_out: bfloat16 [2, 8192, 768], P(None, ('wide', 'narrow'))
- grad_input: bfloat16 [2, 8192, 768], P(None, ('wide', 'narrow'))
- grad_qkv: float32 [768, 2304], P('wide', 'narrow')
- grad_out: float32 [768, 768], P('wide', 'narrow')
- grad_gate: float32 [768, 3072], P('wide', 'narrow')
- grad_up: float32 [768, 3072], P('wide', 'narrow')
- grad_down: float32 [3072, 768], P('wide', 'narrow')
- grad_norms: float32 [4, 768], P('narrow', 'wide')
The draws below stay inside these ranges and needn't reach their ends.
Inputs may be any that keep to these rules, and one draw needn't show every extreme that they name: Each sequence's valid tokens are the first lengths[s] of its 8192 slots; in every draw one sequence has all 8192 valid.
All inputs are finite; a program needn't handle non-finite values.
Results may differ from the reference program's by a relative error of at most 0.035.
Values may be sent and summed in bfloat16 or wider, within the bound.
No kernel may reach another device: no remote copies, remote signals or barrier semaphores. Data moves between devices by JAX's collectives and lax.ppermute only.
A program may use at most 192 MiB of HBM per device.

```python
import jax
import jax.numpy as jnp
from jax import lax

D = 768
HEADS = 12
HEAD = 64
FF = 3072
NORMS = 4
SEQS = 2
LEN = 8192


def draw_lengths(key, part):
    key = jax.random.fold_in(key, 11)
    first_key, second_key = jax.random.split(key)
    drawn = jax.random.randint(first_key, (SEQS,), LEN // 4, LEN + 1)
    chosen = jax.random.randint(second_key, (), 0, SEQS)
    return jnp.where(jnp.arange(SEQS) == chosen, LEN, drawn).astype(jnp.int32)


def shard_levels(stream_key, shape, cuts, low, largest):
    gain, own = 1.0, jax.random.fold_in(stream_key, 6)
    for position, blocks in cuts:
        steps = jnp.exp(jax.random.uniform(jax.random.fold_in(own, position), (blocks,), jnp.float32, low / len(cuts), largest / len(cuts)))
        gain = gain * jnp.repeat(steps, shape[position] // blocks).reshape([-1 if axis == position else 1 for axis in range(len(shape))])
    return gain


def scatter_about(own_key, dims, width, reach, pieces=(), kind=jnp.bfloat16):
    values = width * jax.random.normal(own_key, dims, jnp.float32)
    if pieces:
        values = values * shard_levels(own_key, dims, pieces, -0.22, 0.18)
    return jnp.clip(values, -reach, reach).astype(kind)


def setup_inputs(seed: int = 0) -> dict:
    key_of = jax.random.split(jax.random.key(seed), 10)
    return {
        "hidden_in": scatter_about(key_of[0], (SEQS, LEN, D), 1.0, 6.0, ((1, 128),)),
        "lengths": draw_lengths(jax.random.fold_in(key_of[9], 71), 0),
        "w_qkv": scatter_about(key_of[2], (D, 3 * D), (D // 2) ** -0.5, 0.3125, ((0, 32), (1, 4))),
        "w_out": scatter_about(key_of[3], (D, D), (D // 64) ** -0.5, 1.75, ((0, 32), (1, 4))),
        "w_gate": scatter_about(key_of[4], (D, FF), D ** -0.5, 0.21875, ((0, 32), (1, 4))),
        "w_up": scatter_about(key_of[5], (D, FF), D ** -0.5, 0.21875, ((0, 32), (1, 4))),
        "w_down": scatter_about(key_of[6], (FF, D), (FF // 4) ** -0.5, 0.21875, ((0, 32), (1, 4))),
        "norm_params": jnp.clip(1.0 + 0.1 * jax.random.normal(key_of[7], (NORMS, D), jnp.float32), 0.5, 1.5).astype(jnp.bfloat16),
        "cotangent": scatter_about(key_of[8], (SEQS, LEN, D), 1.0, 6.0, ((1, 128),)),
    }


EPSILON = 1e-05
PRECISE = lax.Precision.HIGHEST

@jax.custom_vjp
def low(v):
    return lax.optimization_barrier(v.astype(jnp.bfloat16)).astype(jnp.float32)

@jax.custom_vjp
def low_back(v):
    return v

def low_keep(v):
    return (low(v), None)

def low_pass(kept, grad):
    return (grad,)

def back_keep(v):
    return (v, None)

def back_low(kept, grad):
    return (low(grad),)
low.defvjp(low_keep, low_pass)
low_back.defvjp(back_keep, back_low)

def rope_tables(positions, head_size):
    freqs = 10000.0 ** (-2.0 * jnp.arange(head_size // 2, dtype=jnp.float32) / head_size)
    angles = positions.astype(jnp.float32)[:, None] * freqs[None, :]
    cosine_table = jnp.cos(angles)
    sine_table = jnp.sin(angles)
    return (jnp.concatenate([cosine_table, cosine_table], -1), jnp.concatenate([sine_table, sine_table], -1))

def rotate(values, cosine_table, sine_table):
    half_width = values.shape[-1] // 2
    turned = jnp.concatenate([-values[..., half_width:], values[..., :half_width]], -1)
    return values * cosine_table + turned * sine_table

def layer_norm(residual, gain_vec, bias_vec):
    row_mean = lax.optimization_barrier(jnp.mean(residual, -1, keepdims=True))
    centred = residual - row_mean
    variance = lax.optimization_barrier(jnp.mean(centred * centred, -1, keepdims=True))
    return centred * lax.rsqrt(variance + EPSILON) * gain_vec + bias_vec

def query_block(query_rows, key_all, value_all, valid_keys):
    scores = jnp.einsum('qhd,khd->hqk', query_rows, key_all, precision=PRECISE) * HEAD ** (-0.5)
    scores = low_back(scores)
    scores = jnp.where(valid_keys[None, None, :], scores, -1e+30)
    probs = low(jax.nn.softmax(scores, axis=-1))
    return jnp.einsum('hqk,khd->qhd', probs, value_all, precision=PRECISE)

def attend(query_all, key_all, value_all, valid_keys):
    block_rows = min(512, LEN)
    block_count = LEN // block_rows
    checked = jax.checkpoint(query_block)
    result = lax.map(lambda rows_in: checked(rows_in, key_all, value_all, valid_keys), query_all.reshape(block_count, block_rows, HEADS, HEAD))
    return result.reshape(LEN, D)

def layer(w_qkv, w_out, w_gate, w_up, w_down, norm_values, tokens, length):
    positions = jnp.arange(LEN, dtype=jnp.int32)
    valid_keys = positions < length
    projected = low_back(jnp.dot(tokens, w_qkv, precision=PRECISE))
    cosine_table, sine_table = rope_tables(positions, HEAD)
    cosine_table = cosine_table[:, None, :]
    sine_table = sine_table[:, None, :]
    query_all = low(rotate(projected[:, :D].reshape(LEN, HEADS, HEAD), cosine_table, sine_table))
    key_all = low(rotate(projected[:, D:2 * D].reshape(LEN, HEADS, HEAD), cosine_table, sine_table))
    value_all = low(projected[:, 2 * D:].reshape(LEN, HEADS, HEAD))
    attended = attend(query_all, key_all, value_all, valid_keys)
    attn_sent = low_back(low(attended))
    projection = low_back(jnp.dot(attn_sent, w_out, precision=PRECISE))
    normed = layer_norm(tokens + projection, norm_values[0], norm_values[1])
    normed_low = low(normed)
    gate_pre = low_back(jnp.dot(normed_low, w_gate, precision=PRECISE))
    up_pre = low_back(jnp.dot(normed_low, w_up, precision=PRECISE))
    activated = low(jax.nn.silu(gate_pre) * up_pre)
    down_out = low_back(jnp.dot(activated, w_down, precision=PRECISE))
    result = layer_norm(normed + down_out, norm_values[2], norm_values[3])
    return result * valid_keys[:, None].astype(jnp.float32)

def reference(hidden_in, lengths, w_qkv, w_out, w_gate, w_up, w_down, norm_params, cotangent):
    weights = (w_qkv.astype(jnp.float32), w_out.astype(jnp.float32), w_gate.astype(jnp.float32), w_up.astype(jnp.float32), w_down.astype(jnp.float32), norm_params.astype(jnp.float32))

    def per_sequence(grad_sums, item):
        tokens, length, incoming = item
        result, pullback = jax.vjp(lambda a, b, c, e, f, g, z: layer(a, b, c, e, f, g, z, length), *weights, tokens)
        grads = pullback(incoming)
        updated = tuple((total_part + grad_part for total_part, grad_part in zip(grad_sums, grads[:6])))
        return (updated, (result.astype(jnp.bfloat16), grads[6].astype(jnp.bfloat16)))
    zero_grads = tuple((jnp.zeros_like(member) for member in weights))
    grad_sums, (layer_outs, input_grads) = lax.scan(per_sequence, zero_grads, (hidden_in.astype(jnp.float32), lengths, cotangent.astype(jnp.float32)))
    return (layer_outs, input_grads, grad_sums[0], grad_sums[1], grad_sums[2], grad_sums[3], grad_sums[4], grad_sums[5])
```

```python
import functools
import math

import jax
import jax.numpy as jnp
from jax import lax
from jax.experimental import pallas as pl
from jax.experimental.pallas import tpu as pltpu
from jax.sharding import Mesh
from jax.sharding import PartitionSpec as P

HEADS = 12
HEAD = 64
EPSILON = 1e-05
AXES = ("y", "z", "xh", "xl", "c")
WIDE = ("y", "z", "xh")
NARROW = ("xl", "c")
QAX = ("z", "xh")
KAX = ("y",)
NQ = 8
NK = 4
LOG2E = math.log2(math.e)
NEG = -1e30
f32 = jnp.float32
bf16 = jnp.bfloat16


def exchange(x, axes):
    return lax.all_to_all(x, axes, 0, 0, tiled=True)


def gather(x, axes, n):
    return exchange(jnp.broadcast_to(x[None], (n,) + x.shape), axes)


def flip(x, axis):
    return lax.ppermute(x, axis, [(0, 1), (1, 0)])


def layer_norm_parts(residual, gain_vec, bias_vec):
    row_mean = jnp.mean(residual, -1, keepdims=True)
    centred = residual - row_mean
    variance = jnp.mean(centred * centred, -1, keepdims=True)
    inv_std = lax.rsqrt(variance + EPSILON)
    unit_rows = centred * inv_std
    return (unit_rows * gain_vec + bias_vec, unit_rows, inv_std)


def norm_back(incoming, unit_rows, inv_std, gain_vec):
    scaled = incoming * gain_vec
    return inv_std * (
        scaled
        - jnp.mean(scaled, -1, keepdims=True)
        - unit_rows * jnp.mean(scaled * unit_rows, -1, keepdims=True)
    )


def sum_to_own(part):
    seqs, slots, width = part.shape
    cells = part.reshape(seqs, 2, 2, slots // 4, width)
    ci, xi = lax.axis_index("c"), lax.axis_index("xl")
    mine = lax.dynamic_index_in_dim(cells, ci, 2, keepdims=False)
    theirs = lax.dynamic_index_in_dim(cells, 1 - ci, 2, keepdims=False)
    half = mine.astype(f32) + flip(theirs.astype(bf16), "c").astype(f32)
    mine = lax.dynamic_index_in_dim(half, xi, 1, keepdims=False)
    theirs = lax.dynamic_index_in_dim(half, 1 - xi, 1, keepdims=False)
    return mine + flip(theirs.astype(bf16), "xl").astype(f32)


def narrow_gather(x):
    return lax.all_gather(x, NARROW, axis=1, tiled=True)


def split3(x):
    hi = x.astype(bf16)
    rest = x - hi.astype(f32)
    mid = rest.astype(bf16)
    low = (rest - mid.astype(f32)).astype(bf16)
    return hi, mid, low


def key_bias(lens_ref, start_ref, seq, tile):
    slot = start_ref[tile] + lax.broadcasted_iota(jnp.int32, (16, 256), 1)
    row = lax.broadcasted_iota(jnp.int32, (16, 256), 0)
    bias = jnp.where(slot < lens_ref[seq], 0.0, NEG)
    return jnp.where(row == 0, bias, jnp.where(row < 4, 1.0, 0.0)).astype(bf16)


def valid_tiles(lens_ref, start_ref, seq):
    n = jnp.int32(0)
    for tile in range(NK):
        n = n + (start_ref[tile] < lens_ref[seq]).astype(jnp.int32)
    return n


def attend_kernel(lens_ref, start_ref, q_ref, kv_ref, out_ref, kx_ref, vx_ref, o_ref, m_ref):
    row = lax.broadcasted_iota(jnp.int32, (16, 256), 0)
    one_row = jnp.where(row == 0, 1.0, 0.0).astype(bf16)
    for seq in range(2):
        for tile in range(NK):
            extra = key_bias(lens_ref, start_ref, seq, tile)
            for h in range(3):
                kt = jnp.concatenate([kv_ref[tile, seq, pl.ds(64 * h, 64), :], extra], 0)
                kx_ref[tile, seq, h] = jnp.transpose(kt)
                vx_ref[tile, seq, h, pl.ds(0, 64), :] = kv_ref[tile, seq, pl.ds(192 + 64 * h, 64), :]
                vx_ref[tile, seq, h, pl.ds(64, 16), :] = one_row
    for seq in range(2):
        tiles = valid_tiles(lens_ref, start_ref, seq)

        @pl.loop(0, NQ)
        def _(block):
            qx = [
                jnp.concatenate([q_ref[block, seq, pl.ds(64 * h, 64), :], one_row], 0)
                for h in range(3)
            ]

            def step(tile, first):
                for h in range(3):
                    s = jnp.dot(kx_ref[tile, seq, h], qx[h], preferred_element_type=f32)
                    peak = jnp.max(s, 0, keepdims=True)
                    if not first:
                        before = m_ref[h, pl.ds(0, 1), :]
                        peak = jnp.maximum(before, peak)
                    p = jnp.exp2(s - peak).astype(bf16)
                    o = jnp.dot(vx_ref[tile, seq, h], p, preferred_element_type=f32)
                    if not first:
                        o = o + o_ref[h] * jnp.exp2(before - peak)
                    o_ref[h] = o
                    m_ref[h, pl.ds(0, 1), :] = peak

            step(0, True)

            @pl.loop(1, tiles)
            def _(tile):
                step(tile, False)

            rows = []
            for h in range(3):
                total = o_ref[h, pl.ds(64, 1), :]
                out_ref[block, seq, pl.ds(64 * h, 64), :] = (
                    o_ref[h, pl.ds(0, 64), :] / total
                ).astype(bf16)
                lse = m_ref[h, pl.ds(0, 1), :] + jnp.log2(total)
                rows += [part.astype(f32) for part in split3(lse)]
            rows.append(jnp.zeros((7, 256), f32))
            out_ref[block, seq, pl.ds(192, 16), :] = jnp.concatenate(rows, 0).astype(bf16)


def attend_back_kernel(
    lens_ref, start_ref, q_ref, kv_ref, g_ref, dq_ref, dkv_ref, kx_ref, vx_ref, dk_ref, dv_ref, acc_ref
):
    row = lax.broadcasted_iota(jnp.int32, (16, 256), 0)
    ones = jnp.where(row < 3, 1.0, 0.0).astype(bf16)
    for seq in range(2):
        for tile in range(NK):
            extra = key_bias(lens_ref, start_ref, seq, tile)
            for h in range(3):
                kt = jnp.concatenate([kv_ref[tile, seq, pl.ds(64 * h, 64), :], extra], 0)
                kx_ref[tile, seq, h] = jnp.transpose(kt)
                vt = jnp.concatenate([kv_ref[tile, seq, pl.ds(192 + 64 * h, 64), :], ones], 0)
                vx_ref[tile, seq, h] = jnp.transpose(vt)
    dk_ref[...] = jnp.zeros_like(dk_ref)
    dv_ref[...] = jnp.zeros_like(dv_ref)
    nt = (((1,), (1,)), ((), ()))
    for seq in range(2):
        tiles = valid_tiles(lens_ref, start_ref, seq)

        @pl.loop(0, NQ)
        def _(block):
            stats = g_ref[block, seq, pl.ds(192, 32), :].astype(f32)
            one = jnp.ones((1, 256), f32)
            q, g, qx, gx = [], [], [], []
            for h in range(3):
                q.append(q_ref[block, seq, pl.ds(64 * h, 64), :])
                g.append(g_ref[block, seq, pl.ds(64 * h, 64), :])
                extra = jnp.concatenate(
                    [one, stats[3 * h : 3 * h + 3], jnp.zeros((12, 256), f32)], 0
                ).astype(bf16)
                qx.append(jnp.concatenate([q[h], extra], 0))
                extra = jnp.concatenate(
                    [stats[16 + 3 * h : 16 + 3 * h + 3], jnp.zeros((13, 256), f32)], 0
                ).astype(bf16)
                gx.append(jnp.concatenate([g[h], extra], 0))

            acc_ref[...] = jnp.zeros_like(acc_ref)

            @pl.loop(0, tiles)
            def _(tile):
                for h in range(3):
                    s = jnp.dot(kx_ref[tile, seq, h], qx[h], preferred_element_type=f32)
                    p = jnp.exp2(s)
                    d = jnp.dot(vx_ref[tile, seq, h], gx[h], preferred_element_type=f32)
                    ds = (p * d).astype(bf16)
                    acc_ref[h] += jnp.dot(
                        kv_ref[tile, seq, pl.ds(64 * h, 64), :], ds, preferred_element_type=f32
                    )
                    dk_ref[tile, seq, h] += lax.dot_general(
                        q[h], ds, nt, preferred_element_type=f32
                    )
                    dv_ref[tile, seq, h] += lax.dot_general(
                        g[h], p.astype(bf16), nt, preferred_element_type=f32
                    )

            for h in range(3):
                dq_ref[block, seq, pl.ds(64 * h, 64), :] = (acc_ref[h] * HEAD**-0.5).astype(bf16)

    for seq in range(2):
        for tile in range(NK):
            for h in range(3):
                dkv_ref[tile, seq, pl.ds(64 * h, 64), :] = (
                    dk_ref[tile, seq, h] * (1.0 / LOG2E)
                ).astype(bf16)
                dkv_ref[tile, seq, pl.ds(192 + 64 * h, 64), :] = dv_ref[tile, seq, h].astype(bf16)


SMEM = pl.BlockSpec(memory_space=pltpu.SMEM)
VMEM = pl.BlockSpec(memory_space=pltpu.VMEM)
PARAMS = pltpu.CompilerParams(vmem_limit_bytes=48 * 1024 * 1024)


def attend(lengths, starts, q_all, kv_all):
    return pl.pallas_call(
        attend_kernel,
        out_shape=jax.ShapeDtypeStruct((NQ, 2, 208, 256), bf16),
        in_specs=[SMEM, SMEM, VMEM, VMEM],
        out_specs=VMEM,
        scratch_shapes=[
            pltpu.VMEM((NK, 2, 3, 256, 80), bf16),
            pltpu.VMEM((NK, 2, 3, 80, 256), bf16),
            pltpu.VMEM((3, 80, 256), f32),
            pltpu.VMEM((3, 8, 256), f32),
        ],
        compiler_params=PARAMS,
        cost_estimate=pl.CostEstimate(
            flops=12_582_912 * 512, bytes_accessed=5_000_000, transcendentals=12_582_912
        ),
    )(lengths, starts, q_all, kv_all)


def attend_back(lengths, starts, q_all, kv_all, g_all):
    return pl.pallas_call(
        attend_back_kernel,
        out_shape=(
            jax.ShapeDtypeStruct((NQ, 2, 192, 256), bf16),
            jax.ShapeDtypeStruct((NK, 2, 384, 256), bf16),
        ),
        in_specs=[SMEM, SMEM, VMEM, VMEM, VMEM],
        out_specs=(VMEM, VMEM),
        scratch_shapes=[
            pltpu.VMEM((NK, 2, 3, 256, 80), bf16),
            pltpu.VMEM((NK, 2, 3, 256, 80), bf16),
            pltpu.VMEM((NK, 2, 3, 64, 256), f32),
            pltpu.VMEM((NK, 2, 3, 64, 256), f32),
            pltpu.VMEM((3, 64, 256), f32),
        ],
        compiler_params=PARAMS,
        cost_estimate=pl.CostEstimate(
            flops=12_582_912 * 1280, bytes_accessed=8_000_000, transcendentals=12_582_912
        ),
    )(lengths, starts, q_all, kv_all, g_all)


def on_device(hidden_in, lengths, w_qkv, w_out, w_gate, w_up, w_down, norm_params, cotangent):
    y_i, z_i, xh_i = (lax.axis_index(a) for a in WIDE)
    wide_i = (y_i * 4 + z_i) * 2 + xh_i
    n_i = lax.axis_index("xl") * 2 + lax.axis_index("c")
    seqs, own_slots, width = hidden_in.shape
    slots = own_slots * 4

    blocks = w_qkv.reshape(24, 3, 192).transpose(1, 0, 2)
    picks = (jnp.arange(4) - 3 * n_i) % 4
    sent = jnp.take(blocks, jnp.minimum(picks, 2), axis=0)
    got = exchange(sent, NARROW)
    sources = (4 * jnp.arange(3) + n_i) // 3
    qkv_mine = jnp.take(got, sources, axis=0).transpose(1, 0, 2).reshape(24, 576)
    wqkv = gather(qkv_mine, WIDE, 32).reshape(width, 576)

    turn_pairs = [
        ((y * 4 + n), (n * 4 + y)) for y in range(4) for n in range(4)
    ]
    down_turned = lax.ppermute(w_down, ("y",) + NARROW, turn_pairs)
    out_rows = narrow_gather(w_out)
    norm_rows = lax.all_gather(norm_params, NARROW, axis=0, tiled=True)
    norm_row = jnp.pad(norm_rows.reshape(1, 96), ((0, 7), (0, width - 96)))
    packed = jnp.concatenate(
        [w_gate, w_up, out_rows, down_turned.reshape(24, width), norm_row], axis=0
    )
    all_weights = gather(packed, WIDE, 32)
    wgate = all_weights[:, 0:24].reshape(width, width)
    wup = all_weights[:, 24:48].reshape(width, width)
    wout = all_weights[:, 48:72].reshape(width, width)
    wdown = (
        all_weights[:, 72:96].reshape(4, 8, 96, 192).transpose(1, 2, 0, 3).reshape(width, width)
    )
    norm_values = (
        all_weights[:, 96, :96].reshape(32, 4, 24).transpose(1, 0, 2).reshape(4, width).astype(f32)
    )

    tokens = narrow_gather(hidden_in)
    positions = wide_i * slots + jnp.arange(slots)
    freqs = 10000.0 ** (-2.0 * jnp.arange(HEAD // 2, dtype=f32) / HEAD)
    angles = freqs[:, None] * positions.astype(f32)[None, :]
    cosine, sine = jnp.cos(angles), jnp.sin(angles)
    projected = jnp.einsum("df,std->sft", wqkv, tokens, preferred_element_type=f32)

    def rotate(block):
        halves = block.reshape(seqs, 3, 2, HEAD // 2, slots)
        first, second = halves[:, :, 0], halves[:, :, 1]
        return jnp.stack(
            [first * cosine - second * sine, second * cosine + first * sine], 2
        ).reshape(seqs, 192, slots)

    query = (rotate(projected[:, :192]) * (HEAD**-0.5 * LOG2E)).astype(bf16)
    keyval = jnp.concatenate(
        [rotate(projected[:, 192:384]), projected[:, 384:]], axis=1
    ).astype(bf16)
    q_all = gather(query, QAX, NQ)
    kv_all = gather(keyval, KAX, NK)
    starts = (jnp.arange(NK) * 8 + z_i * 2 + xh_i).astype(jnp.int32) * slots
    parts = attend(lengths, starts, q_all, kv_all)
    parts = exchange(parts, QAX).astype(f32)
    part_lse = jnp.sum(parts[:, :, 192:201].reshape(NQ, seqs, 3, 3, slots), 3)
    top = jnp.max(part_lse, 0)
    lse = top + jnp.log2(jnp.sum(jnp.exp2(part_lse - top), 0))
    shares = jnp.exp2(part_lse - lse)
    attended = jnp.sum(
        parts[:, :, :192].reshape(NQ, seqs, 3, HEAD, slots) * shares[:, :, :, None, :], 0
    )
    attn_sent = attended.reshape(seqs, 192, slots).astype(bf16)
    attn_all = narrow_gather(attn_sent)

    projection = jnp.einsum("sft,fd->std", attn_all, wout, preferred_element_type=f32)
    normed, _, _ = layer_norm_parts(
        tokens.astype(f32) + projection, norm_values[0], norm_values[1]
    )
    normed_low = normed.astype(bf16)
    own_slice = lambda a: lax.dynamic_slice_in_dim(a, n_i * own_slots, own_slots, 1)
    own_first, unit_first, inv_first = layer_norm_parts(
        hidden_in.astype(f32) + own_slice(projection), norm_values[0], norm_values[1]
    )
    flat_low = normed_low.reshape(-1, width)
    gate_pre = jnp.dot(flat_low, wgate, preferred_element_type=f32)
    up_pre = jnp.dot(flat_low, wup, preferred_element_type=f32)
    gate_sigmoid = jax.nn.sigmoid(gate_pre)
    gate_silu = gate_pre * gate_sigmoid
    activated = (gate_silu * up_pre).astype(bf16)
    down_part = jnp.dot(activated, wdown, preferred_element_type=f32)
    down_out = sum_to_own(down_part.reshape(seqs, slots, width))
    output_rows, unit_second, inv_second = layer_norm_parts(
        own_first + down_out, norm_values[2], norm_values[3]
    )
    own_positions = wide_i * slots + n_i * own_slots + jnp.arange(own_slots)
    valid = (own_positions[None, :] < lengths[:, None]).astype(f32)[:, :, None]
    layer_out = (output_rows * valid).astype(bf16)
    grad_rows = cotangent.astype(f32) * valid
    grad_gain2 = jnp.sum(grad_rows * unit_second, (0, 1))
    grad_bias2 = jnp.sum(grad_rows, (0, 1))
    grad_second = norm_back(grad_rows, unit_second, inv_second, norm_values[2])
    down_low = narrow_gather(grad_second.astype(bf16)).reshape(-1, width)

    grad_wdown = jnp.einsum("tf,td->fd", activated, down_low, preferred_element_type=f32)
    grad_act = jnp.einsum("td,fd->tf", down_low, wdown, preferred_element_type=f32)
    silu_slope = gate_sigmoid * (1.0 + gate_pre * (1.0 - gate_sigmoid))
    grad_gate_low = (grad_act * up_pre * silu_slope).astype(bf16)
    grad_up_low = (grad_act * gate_silu).astype(bf16)
    grad_wgate = jnp.einsum("td,tf->df", flat_low, grad_gate_low, preferred_element_type=f32)
    grad_wup = jnp.einsum("td,tf->df", flat_low, grad_up_low, preferred_element_type=f32)
    first_part = jnp.einsum(
        "tf,df->td", grad_gate_low, wgate, preferred_element_type=f32
    ) + jnp.einsum("tf,df->td", grad_up_low, wup, preferred_element_type=f32)
    grad_normed = grad_second + sum_to_own(first_part.reshape(seqs, slots, width))
    grad_gain1 = jnp.sum(grad_normed * unit_first, (0, 1))
    grad_bias1 = jnp.sum(grad_normed, (0, 1))
    grad_first = norm_back(grad_normed, unit_first, inv_first, norm_values[0])
    res_low = narrow_gather(grad_first.astype(bf16))
    out_mine = lax.dynamic_slice_in_dim(wout, n_i * 192, 192, 0)
    grad_attn = jnp.einsum("fd,std->sft", out_mine, res_low, preferred_element_type=f32).astype(
        bf16
    )
    delta = jnp.sum(
        grad_attn.astype(f32).reshape(seqs, 3, HEAD, slots) * attended, 2
    )

    def three(x):
        hi = lax.reduce_precision(x, 8, 7)
        mid = lax.reduce_precision(x - hi, 8, 7)
        low = x - hi - mid
        return jnp.pad(
            jnp.stack([hi, mid, low], 2).reshape(seqs, 9, slots), ((0, 0), (0, 7), (0, 0))
        )

    sent_back = jnp.concatenate(
        [grad_attn, three(-lse).astype(bf16), three(-delta).astype(bf16)], axis=1
    )
    g_all = gather(sent_back, QAX, NQ)

    res_cols = lax.dynamic_slice_in_dim(res_low, n_i * 192, 192, 2)
    grad_wout = jnp.einsum("sft,std->fd", attn_all, res_cols, preferred_element_type=f32)
    grad_norm_rows = jnp.stack([grad_gain1, grad_bias1, grad_gain2, grad_bias2])
    norm_blocks = grad_norm_rows.reshape(4, 32, 24).transpose(1, 0, 2).reshape(32, 1, 96)
    norm_blocks = jnp.pad(norm_blocks, ((0, 0), (0, 1), (0, width - 96)))
    grads_packed = jnp.concatenate(
        [
            grad_wgate.reshape(32, 24, width),
            grad_wup.reshape(32, 24, width),
            grad_wdown.reshape(8, 96, 4, 192).transpose(2, 0, 1, 3).reshape(32, 24, width),
            grad_wout.reshape(32, 6, width),
            norm_blocks,
        ],
        axis=1,
    ).astype(bf16)
    grads_got = jnp.sum(exchange(grads_packed, WIDE).astype(f32), 0)
    sum_gate = grads_got[0:24]
    sum_up = grads_got[24:48]
    sum_down = lax.ppermute(
        grads_got[48:72].reshape(96, 192).astype(bf16), ("y",) + NARROW, turn_pairs
    ).astype(f32)
    sum_out = grads_got[72:78].reshape(24, 192)
    norm_sums = grads_got[78, :96].reshape(4, 24)

    dq_parts, dkv_parts = attend_back(lengths, starts, q_all, kv_all, g_all)
    grad_query = jnp.sum(exchange(dq_parts, QAX).astype(f32), 0)
    grad_keyval = jnp.sum(exchange(dkv_parts, KAX).astype(f32), 0)

    def unrotate(block):
        halves = block.reshape(seqs, 3, 2, HEAD // 2, slots)
        first, second = halves[:, :, 0], halves[:, :, 1]
        return jnp.stack(
            [first * cosine + second * sine, second * cosine - first * sine], 2
        ).reshape(seqs, 192, slots)

    grad_proj = jnp.concatenate(
        [unrotate(grad_query), unrotate(grad_keyval[:, :192]), grad_keyval[:, 192:]], axis=1
    ).astype(bf16)
    grad_wqkv = jnp.einsum("std,sft->df", tokens, grad_proj, preferred_element_type=f32)
    input_part = jnp.einsum("sft,df->std", grad_proj, wqkv, preferred_element_type=f32)
    grad_input = (grad_first + sum_to_own(input_part)).astype(bf16)
    qkv_got = jnp.sum(
        exchange(grad_wqkv.reshape(32, 24, 576).astype(bf16), WIDE).astype(f32), 0
    )
    back = qkv_got.reshape(24, 3, 192).transpose(1, 0, 2)
    where = (sources[None, :] == jnp.arange(4)[:, None]).astype(f32)
    back_sent = jnp.einsum("sk,kdf->sdf", where, back)
    norm_sent = jnp.pad(norm_sums[:, None, :], ((0, 0), (0, 7), (0, 168)))
    back_got = exchange(jnp.concatenate([back_sent, norm_sent], 1).astype(bf16), NARROW).astype(f32)
    sum_norms = jnp.sum(back_got[:, 24, :24], 0)[None]
    order = (3 * n_i + jnp.arange(3)) % 4
    sum_qkv = jnp.take(back_got[:, :24], order, axis=0).transpose(1, 0, 2).reshape(24, 576)
    return (layer_out, grad_input, sum_qkv, sum_out, sum_gate, sum_up, sum_down, sum_norms)


def solution(mesh):
    fine = Mesh(mesh.devices.reshape(4, 4, 2, 2, 2), AXES)
    token = P(None, WIDE + NARROW, None)
    weight = P(WIDE, NARROW)
    norm = P(NARROW, WIDE)
    return jax.shard_map(
        on_device,
        mesh=fine,
        in_specs=(token, P(), weight, weight, weight, weight, weight, norm, token),
        out_specs=(token, token, weight, weight, weight, weight, weight, norm),
        check_vma=False,
    )
```

```python
import functools
import math

import jax
import jax.numpy as jnp
from jax import lax
from jax.experimental import pallas as pl
from jax.experimental.pallas import tpu as pltpu
from jax.sharding import Mesh
from jax.sharding import PartitionSpec as P

HEADS = 12
HEAD = 64
EPSILON = 1e-05
AXES = ("y", "z", "xh", "xl", "c")
WIDE = ("y", "z", "xh")
NARROW = ("xl", "c")
QAX = ("z", "xh")
KAX = ("y",)
NQ = 8
NK = 4
STEP = 4
LOG2E = math.log2(math.e)
NEG = -1e30
f32 = jnp.float32
bf16 = jnp.bfloat16


def exchange(x, axes):
    return lax.all_to_all(x, axes, 0, 0, tiled=True)


def gather(x, axes, n):
    return exchange(jnp.broadcast_to(x[None], (n,) + x.shape), axes)


def flip(x, axis):
    return lax.ppermute(x, axis, [(0, 1), (1, 0)])


def layer_norm_parts(residual, gain_vec, bias_vec):
    row_mean = jnp.mean(residual, -1, keepdims=True)
    centred = residual - row_mean
    variance = jnp.mean(centred * centred, -1, keepdims=True)
    inv_std = lax.rsqrt(variance + EPSILON)
    unit_rows = centred * inv_std
    return (unit_rows * gain_vec + bias_vec, unit_rows, inv_std)


def norm_back(incoming, unit_rows, inv_std, gain_vec):
    scaled = incoming * gain_vec
    return inv_std * (
        scaled
        - jnp.mean(scaled, -1, keepdims=True)
        - unit_rows * jnp.mean(scaled * unit_rows, -1, keepdims=True)
    )


def sum_to_own(part):
    seqs, slots, width = part.shape
    cells = part.reshape(seqs, 2, 2, slots // 4, width)
    ci, xi = lax.axis_index("c"), lax.axis_index("xl")
    mine = lax.dynamic_index_in_dim(cells, ci, 2, keepdims=False)
    theirs = lax.dynamic_index_in_dim(cells, 1 - ci, 2, keepdims=False)
    half = mine.astype(f32) + flip(theirs.astype(bf16), "c").astype(f32)
    mine = lax.dynamic_index_in_dim(half, xi, 1, keepdims=False)
    theirs = lax.dynamic_index_in_dim(half, 1 - xi, 1, keepdims=False)
    return mine + flip(theirs.astype(bf16), "xl").astype(f32)


def narrow_gather(x):
    return lax.all_gather(x, NARROW, axis=1, tiled=True)


def split3(x):
    hi = x.astype(bf16)
    rest = x - hi.astype(f32)
    mid = rest.astype(bf16)
    low = (rest - mid.astype(f32)).astype(bf16)
    return hi, mid, low


def key_bias(lens_ref, start_ref, seq, tile):
    slot = start_ref[tile] + lax.broadcasted_iota(jnp.int32, (16, 256), 1)
    row = lax.broadcasted_iota(jnp.int32, (16, 256), 0)
    bias = jnp.where(slot < lens_ref[seq], 0.0, NEG)
    return jnp.where(row == 0, bias, jnp.where(row < 4, 1.0, 0.0)).astype(bf16)


def valid_tiles(lens_ref, start_ref, seq):
    n = jnp.int32(0)
    for tile in range(NK):
        n = n + (start_ref[tile] < lens_ref[seq]).astype(jnp.int32)
    return n


def pick_tiles(lens_ref, start_ref, seq, run):
    n = valid_tiles(lens_ref, start_ref, seq)
    for tiles in range(1, NK + 1):
        pl.when(n == tiles)(functools.partial(run, seq, tiles))


def attend_kernel(lens_ref, start_ref, q_ref, kv_ref, out_ref, kx_ref, vx_ref, sum_ref, peak_ref):
    row = lax.broadcasted_iota(jnp.int32, (16, 256), 0)
    one_row = jnp.where(row == 0, 1.0, 0.0).astype(bf16)
    one_rows = jnp.concatenate([one_row] * STEP, 1)
    for seq in range(2):
        for tile in range(NK):
            extra = key_bias(lens_ref, start_ref, seq, tile)
            here = pl.ds(256 * tile, 256)
            for h in range(3):
                kt = jnp.concatenate([kv_ref[tile, seq, pl.ds(64 * h, 64), :], extra], 0)
                kx_ref[seq, h, here, :] = jnp.transpose(kt)
                vx_ref[seq, h, pl.ds(0, 64), here] = kv_ref[tile, seq, pl.ds(192 + 64 * h, 64), :]
                vx_ref[seq, h, pl.ds(64, 16), here] = one_row

    def run(seq, tiles):
        keys = pl.ds(0, 256 * tiles)

        @pl.loop(0, NQ // STEP)
        def _(turn):
            for h in range(3):
                q = [q_ref[turn * STEP + j, seq, pl.ds(64 * h, 64), :] for j in range(STEP)]
                qx = jnp.concatenate([jnp.concatenate(q, 1), one_rows], 0)
                s = jnp.dot(kx_ref[seq, h, keys, :], qx, preferred_element_type=f32)
                peak = jnp.max(s, 0, keepdims=True)
                p = jnp.exp2(s - peak).astype(bf16)
                o = jnp.dot(vx_ref[seq, h, :, keys], p, preferred_element_type=f32)
                total = o[64:65]
                o = (o[:64] * (1.0 / total)).astype(bf16)
                for j in range(STEP):
                    here = slice(256 * j, 256 * j + 256)
                    out_ref[turn * STEP + j, seq, pl.ds(64 * h, 64), :] = o[:, here]
                    sum_ref[turn * STEP + j, seq, pl.ds(h, 1), :] = total[:, here]
                    peak_ref[turn * STEP + j, seq, pl.ds(h, 1), :] = peak[:, here]

    for seq in range(2):
        pick_tiles(lens_ref, start_ref, seq, run)
    for seq in range(2):
        for block in range(NQ):
            lse = peak_ref[block, seq, pl.ds(0, 3), :] + jnp.log2(sum_ref[block, seq, pl.ds(0, 3), :])
            rows = [part.astype(f32) for part in split3(lse)] + [jnp.zeros((7, 256), f32)]
            out_ref[block, seq, pl.ds(192, 16), :] = jnp.concatenate(rows, 0).astype(bf16)


def attend_back_kernel(
    lens_ref, start_ref, q_ref, kv_ref, g_ref, dq_ref, dkv_ref, kx_ref, vx_ref, kt_ref, dk_ref, dv_ref
):
    row = lax.broadcasted_iota(jnp.int32, (16, 256), 0)
    ones = jnp.where(row < 3, 1.0, 0.0).astype(bf16)
    one = jnp.ones((1, 256), f32)
    nt = (((1,), (1,)), ((), ()))
    for seq in range(2):
        for tile in range(NK):
            extra = key_bias(lens_ref, start_ref, seq, tile)
            here = pl.ds(256 * tile, 256)
            for h in range(3):
                k = kv_ref[tile, seq, pl.ds(64 * h, 64), :]
                v = kv_ref[tile, seq, pl.ds(192 + 64 * h, 64), :]
                kx_ref[seq, h, here, :] = jnp.transpose(jnp.concatenate([k, extra], 0))
                vx_ref[seq, h, here, :] = jnp.transpose(jnp.concatenate([v, ones], 0))
                kt_ref[seq, h, :, here] = k
    dk_ref[...] = jnp.zeros_like(dk_ref)
    dv_ref[...] = jnp.zeros_like(dv_ref)

    def run(seq, tiles):
        keys = pl.ds(0, 256 * tiles)

        @pl.loop(0, NQ)
        def _(block):
            stats = g_ref[block, seq, pl.ds(192, 32), :].astype(f32)
            for h in range(3):
                q = q_ref[block, seq, pl.ds(64 * h, 64), :]
                g = g_ref[block, seq, pl.ds(64 * h, 64), :]
                rows = [one, stats[3 * h : 3 * h + 3], jnp.zeros((12, 256), f32)]
                qx = jnp.concatenate([q, jnp.concatenate(rows, 0).astype(bf16)], 0)
                rows = [stats[16 + 3 * h : 16 + 3 * h + 3], jnp.zeros((13, 256), f32)]
                gx = jnp.concatenate([g, jnp.concatenate(rows, 0).astype(bf16)], 0)
                p = jnp.exp2(jnp.dot(kx_ref[seq, h, keys, :], qx, preferred_element_type=f32))
                d = jnp.dot(vx_ref[seq, h, keys, :], gx, preferred_element_type=f32)
                ds = (p * d).astype(bf16)
                dq = jnp.dot(kt_ref[seq, h, :, keys], ds, preferred_element_type=f32)
                dk_ref[seq, h, :, keys] += lax.dot_general(q, ds, nt, preferred_element_type=f32)
                dv_ref[seq, h, :, keys] += lax.dot_general(
                    g, p.astype(bf16), nt, preferred_element_type=f32
                )
                dq_ref[block, seq, pl.ds(64 * h, 64), :] = (dq * HEAD**-0.5).astype(bf16)

    for seq in range(2):
        pick_tiles(lens_ref, start_ref, seq, run)
    for seq in range(2):
        for tile in range(NK):
            here = pl.ds(256 * tile, 256)
            for h in range(3):
                dk = dk_ref[seq, h, :, here] * (1.0 / LOG2E)
                dkv_ref[tile, seq, pl.ds(64 * h, 64), :] = dk.astype(bf16)
                dkv_ref[tile, seq, pl.ds(192 + 64 * h, 64), :] = dv_ref[seq, h, :, here].astype(bf16)


SMEM = pl.BlockSpec(memory_space=pltpu.SMEM)
VMEM = pl.BlockSpec(memory_space=pltpu.VMEM)
PARAMS = pltpu.CompilerParams(vmem_limit_bytes=56 * 1024 * 1024)


def attend(lengths, starts, q_all, kv_all):
    return pl.pallas_call(
        attend_kernel,
        out_shape=jax.ShapeDtypeStruct((NQ, 2, 208, 256), bf16),
        in_specs=[SMEM, SMEM, VMEM, VMEM],
        out_specs=VMEM,
        scratch_shapes=[
            pltpu.VMEM((2, 3, 1024, 80), bf16),
            pltpu.VMEM((2, 3, 80, 1024), bf16),
            pltpu.VMEM((NQ, 2, 8, 256), f32),
            pltpu.VMEM((NQ, 2, 8, 256), f32),
        ],
        compiler_params=PARAMS,
        cost_estimate=pl.CostEstimate(
            flops=23_000_000_000, bytes_accessed=5_000_000, transcendentals=12_582_912
        ),
    )(lengths, starts, q_all, kv_all)


def attend_back(lengths, starts, q_all, kv_all, g_all):
    return pl.pallas_call(
        attend_back_kernel,
        out_shape=(
            jax.ShapeDtypeStruct((NQ, 2, 192, 256), bf16),
            jax.ShapeDtypeStruct((NK, 2, 384, 256), bf16),
        ),
        in_specs=[SMEM, SMEM, VMEM, VMEM, VMEM],
        out_specs=(VMEM, VMEM),
        scratch_shapes=[
            pltpu.VMEM((2, 3, 1024, 80), bf16),
            pltpu.VMEM((2, 3, 1024, 80), bf16),
            pltpu.VMEM((2, 3, 64, 1024), bf16),
            pltpu.VMEM((2, 3, 64, 1024), f32),
            pltpu.VMEM((2, 3, 64, 1024), f32),
        ],
        compiler_params=PARAMS,
        cost_estimate=pl.CostEstimate(
            flops=46_000_000_000, bytes_accessed=8_000_000, transcendentals=12_582_912
        ),
    )(lengths, starts, q_all, kv_all, g_all)


def on_device(hidden_in, lengths, w_qkv, w_out, w_gate, w_up, w_down, norm_params, cotangent):
    y_i, z_i, xh_i = (lax.axis_index(a) for a in WIDE)
    wide_i = (y_i * 4 + z_i) * 2 + xh_i
    n_i = lax.axis_index("xl") * 2 + lax.axis_index("c")
    seqs, own_slots, width = hidden_in.shape
    slots = own_slots * 4

    blocks = w_qkv.reshape(24, 3, 192).transpose(1, 0, 2)
    picks = jnp.minimum((jnp.arange(4) - 3 * n_i) % 4, 2)
    norm_row = jnp.pad(norm_params, ((0, 7), (0, 168)))
    sent = jnp.concatenate(
        [
            jnp.take(blocks, picks, axis=0),
            jnp.broadcast_to(jnp.concatenate([w_out, norm_row])[None], (4, 32, 192)),
        ],
        axis=1,
    )
    got = exchange(sent, NARROW)
    sources = (4 * jnp.arange(3) + n_i) // 3
    qkv_mine = jnp.take(got[:, :24], sources, axis=0).transpose(1, 0, 2).reshape(24, 576)
    wqkv = gather(qkv_mine, WIDE, 32).reshape(width, 576)

    turn_pairs = [((y * 4 + n), (n * 4 + y)) for y in range(4) for n in range(4)]
    down_turned = lax.ppermute(w_down, ("y",) + NARROW, turn_pairs)
    out_rows = got[:, 24:48].transpose(1, 0, 2).reshape(24, width)
    norm_row = jnp.pad(got[:, 48, :24].reshape(1, 96), ((0, 7), (0, width - 96)))
    packed = jnp.concatenate(
        [w_gate, w_up, out_rows, down_turned.reshape(24, width), norm_row], axis=0
    )
    all_weights = lax.all_gather(packed, WIDE)
    wgate = all_weights[:, 0:24].reshape(width, width)
    wup = all_weights[:, 24:48].reshape(width, width)
    wout = all_weights[:, 48:72].reshape(width, width)
    wdown = (
        all_weights[:, 72:96].reshape(4, 8, 96, 192).transpose(1, 2, 0, 3).reshape(width, width)
    )
    norm_values = (
        all_weights[:, 96, :96].reshape(32, 4, 24).transpose(1, 0, 2).reshape(4, width).astype(f32)
    )

    tokens = narrow_gather(hidden_in)
    positions = wide_i * slots + jnp.arange(slots)
    freqs = 10000.0 ** (-2.0 * jnp.arange(HEAD // 2, dtype=f32) / HEAD)
    angles = freqs[:, None] * positions.astype(f32)[None, :]
    cosine, sine = jnp.cos(angles), jnp.sin(angles)
    projected = jnp.einsum("df,std->sft", wqkv, tokens, preferred_element_type=f32)

    def rotate(block):
        halves = block.reshape(seqs, 3, 2, HEAD // 2, slots)
        first, second = halves[:, :, 0], halves[:, :, 1]
        return jnp.stack(
            [first * cosine - second * sine, second * cosine + first * sine], 2
        ).reshape(seqs, 192, slots)

    query = (rotate(projected[:, :192]) * (HEAD**-0.5 * LOG2E)).astype(bf16)
    keyval = jnp.concatenate(
        [rotate(projected[:, 192:384]), projected[:, 384:]], axis=1
    ).astype(bf16)
    q_all = gather(query, QAX, NQ)
    kv_all = gather(keyval, KAX, NK)
    starts = (jnp.arange(NK) * 8 + z_i * 2 + xh_i).astype(jnp.int32) * slots
    parts = attend(lengths, starts, q_all, kv_all)
    parts = exchange(parts, QAX).astype(f32)
    part_lse = jnp.sum(parts[:, :, 192:201].reshape(NQ, seqs, 3, 3, slots), 2)
    top = jnp.max(part_lse, 0)
    lse = top + jnp.log2(jnp.sum(jnp.exp2(part_lse - top), 0))
    shares = jnp.exp2(part_lse - lse)
    attended = jnp.sum(
        parts[:, :, :192].reshape(NQ, seqs, 3, HEAD, slots) * shares[:, :, :, None, :], 0
    )
    attn_sent = attended.reshape(seqs, 192, slots).astype(bf16)
    attn_all = narrow_gather(attn_sent)

    projection = jnp.einsum("sft,fd->std", attn_all, wout, preferred_element_type=f32)
    normed, _, _ = layer_norm_parts(
        tokens.astype(f32) + projection, norm_values[0], norm_values[1]
    )
    normed_low = normed.astype(bf16)
    own_slice = lambda a: lax.dynamic_slice_in_dim(a, n_i * own_slots, own_slots, 1)
    own_first, unit_first, inv_first = layer_norm_parts(
        hidden_in.astype(f32) + own_slice(projection), norm_values[0], norm_values[1]
    )
    flat_low = normed_low.reshape(-1, width)
    gate_pre = jnp.dot(flat_low, wgate, preferred_element_type=f32)
    up_pre = jnp.dot(flat_low, wup, preferred_element_type=f32)
    gate_sigmoid = jax.nn.sigmoid(gate_pre)
    gate_silu = gate_pre * gate_sigmoid
    activated = (gate_silu * up_pre).astype(bf16)
    down_part = jnp.dot(activated, wdown, preferred_element_type=f32)
    down_out = sum_to_own(down_part.reshape(seqs, slots, width))
    output_rows, unit_second, inv_second = layer_norm_parts(
        own_first + down_out, norm_values[2], norm_values[3]
    )
    own_positions = wide_i * slots + n_i * own_slots + jnp.arange(own_slots)
    valid = (own_positions[None, :] < lengths[:, None]).astype(f32)[:, :, None]
    layer_out = (output_rows * valid).astype(bf16)
    grad_rows = cotangent.astype(f32) * valid
    grad_gain2 = jnp.sum(grad_rows * unit_second, (0, 1))
    grad_bias2 = jnp.sum(grad_rows, (0, 1))
    grad_second = norm_back(grad_rows, unit_second, inv_second, norm_values[2])
    down_low = narrow_gather(grad_second.astype(bf16)).reshape(-1, width)

    grad_wdown = jnp.einsum("tf,td->fd", activated, down_low, preferred_element_type=f32)
    grad_act = jnp.einsum("td,fd->tf", down_low, wdown, preferred_element_type=f32)
    silu_slope = gate_sigmoid * (1.0 + gate_pre * (1.0 - gate_sigmoid))
    grad_gate_low = (grad_act * up_pre * silu_slope).astype(bf16)
    grad_up_low = (grad_act * gate_silu).astype(bf16)
    grad_wgate = jnp.einsum("td,tf->df", flat_low, grad_gate_low, preferred_element_type=f32)
    grad_wup = jnp.einsum("td,tf->df", flat_low, grad_up_low, preferred_element_type=f32)
    first_part = jnp.einsum(
        "tf,df->td", grad_gate_low, wgate, preferred_element_type=f32
    ) + jnp.einsum("tf,df->td", grad_up_low, wup, preferred_element_type=f32)
    grad_normed = grad_second + sum_to_own(first_part.reshape(seqs, slots, width))
    grad_gain1 = jnp.sum(grad_normed * unit_first, (0, 1))
    grad_bias1 = jnp.sum(grad_normed, (0, 1))
    grad_first = norm_back(grad_normed, unit_first, inv_first, norm_values[0])
    res_low = narrow_gather(grad_first.astype(bf16))
    out_mine = lax.dynamic_slice_in_dim(wout, n_i * 192, 192, 0)
    grad_attn = jnp.einsum("fd,std->sft", out_mine, res_low, preferred_element_type=f32).astype(
        bf16
    )
    delta = jnp.sum(
        grad_attn.astype(f32).reshape(seqs, 3, HEAD, slots) * attended, 2
    )

    def three(x):
        hi = lax.reduce_precision(x, 8, 7)
        mid = lax.reduce_precision(x - hi, 8, 7)
        low = x - hi - mid
        return jnp.pad(
            jnp.stack([hi, mid, low], 2).reshape(seqs, 9, slots), ((0, 0), (0, 7), (0, 0))
        )

    sent_back = jnp.concatenate(
        [grad_attn, three(-lse).astype(bf16), three(-delta).astype(bf16)], axis=1
    )
    g_all = gather(sent_back, QAX, NQ)

    grad_norm_rows = jnp.stack([grad_gain1, grad_bias1, grad_gain2, grad_bias2])
    norm_blocks = grad_norm_rows.reshape(4, 32, 24).transpose(1, 0, 2).reshape(32, 1, 96)
    norm_blocks = jnp.pad(norm_blocks, ((0, 0), (0, 7), (0, width - 96))).astype(bf16)
    grads_packed = jnp.concatenate(
        [
            grad_wgate.astype(bf16).reshape(32, 24, width),
            grad_wup.astype(bf16).reshape(32, 24, width),
            grad_wdown.astype(bf16)
            .reshape(8, 96, 4, 192)
            .transpose(2, 0, 1, 3)
            .reshape(32, 24, width),
            norm_blocks,
        ],
        axis=1,
    )
    grads_packed, g_all = lax.optimization_barrier((grads_packed, g_all))
    grads_got = exchange(grads_packed, WIDE)
    dq_parts, dkv_parts = attend_back(lengths, starts, q_all, kv_all, g_all)
    grads_got, dq_parts, dkv_parts = lax.optimization_barrier((grads_got, dq_parts, dkv_parts))
    grads_got = jnp.sum(grads_got.astype(f32), 0)
    sum_gate = grads_got[0:24]
    sum_up = grads_got[24:48]
    sum_down = lax.ppermute(
        grads_got[48:72].reshape(96, 192).astype(bf16), ("y",) + NARROW, turn_pairs
    ).astype(f32)
    norm_sums = grads_got[72, :96].reshape(4, 24)

    grad_query = jnp.sum(exchange(dq_parts, QAX).astype(f32), 0)
    grad_keyval = jnp.sum(exchange(dkv_parts, KAX).astype(f32), 0)

    def unrotate(block):
        halves = block.reshape(seqs, 3, 2, HEAD // 2, slots)
        first, second = halves[:, :, 0], halves[:, :, 1]
        return jnp.stack(
            [first * cosine + second * sine, second * cosine - first * sine], 2
        ).reshape(seqs, 192, slots)

    grad_proj = jnp.concatenate(
        [unrotate(grad_query), unrotate(grad_keyval[:, :192]), grad_keyval[:, 192:]], axis=1
    ).astype(bf16)
    grad_wqkv = jnp.einsum("std,sft->df", tokens, grad_proj, preferred_element_type=f32)
    input_part = jnp.einsum("sft,df->std", grad_proj, wqkv, preferred_element_type=f32)
    grad_input = (grad_first + sum_to_own(input_part)).astype(bf16)
    res_cols = lax.dynamic_slice_in_dim(res_low, n_i * 192, 192, 2)
    grad_wout = jnp.einsum("sft,std->fd", attn_all, res_cols, preferred_element_type=f32)
    last = jnp.concatenate([grad_wqkv.astype(bf16), grad_wout.astype(bf16)], axis=1)
    last_got = jnp.sum(exchange(last.reshape(32, 24, width), WIDE).astype(f32), 0)
    sum_out = last_got[:, 576:]
    back = last_got[:, :576].reshape(24, 3, 192).transpose(1, 0, 2)
    where = (sources[None, :] == jnp.arange(4)[:, None]).astype(f32)
    back_sent = jnp.einsum("sk,kdf->sdf", where, back)
    norm_sent = jnp.pad(norm_sums[:, None, :], ((0, 0), (0, 7), (0, 168)))
    back_got = exchange(jnp.concatenate([back_sent, norm_sent], 1).astype(bf16), NARROW).astype(f32)
    sum_norms = jnp.sum(back_got[:, 24, :24], 0)[None]
    order = (3 * n_i + jnp.arange(3)) % 4
    sum_qkv = jnp.take(back_got[:, :24], order, axis=0).transpose(1, 0, 2).reshape(24, 576)
    return (layer_out, grad_input, sum_qkv, sum_out, sum_gate, sum_up, sum_down, sum_norms)


def solution(mesh):
    fine = Mesh(mesh.devices.reshape(4, 4, 2, 2, 2), AXES)
    token = P(None, WIDE + NARROW, None)
    weight = P(WIDE, NARROW)
    norm = P(NARROW, WIDE)
    return jax.shard_map(
        on_device,
        mesh=fine,
        in_specs=(token, P(), weight, weight, weight, weight, weight, norm, token),
        out_specs=(token, token, weight, weight, weight, weight, weight, norm),
        check_vma=False,
    )
```

```python
import functools
import math

import jax
import jax.numpy as jnp
from jax import lax
from jax.experimental import pallas as pl
from jax.experimental.pallas import tpu as pltpu
from jax.sharding import Mesh
from jax.sharding import PartitionSpec as P

HEADS = 12
HEAD = 64
EPSILON = 1e-05
AXES = ("y", "z", "xh", "xl", "c")
WIDE = ("y", "z", "xh")
NARROW = ("xl", "c")
QAX = ("z", "xh")
NQ = 8
NK = 4
STEP = 4
LOG2E = math.log2(math.e)
NEG = -1e30
f32 = jnp.float32
bf16 = jnp.bfloat16


def exchange(x, axes):
    return lax.all_to_all(x, axes, 0, 0, tiled=True)


def gather(x, axes, n):
    return exchange(jnp.broadcast_to(x[None], (n,) + x.shape), axes)


def along(x, axis, by):
    return lax.ppermute(x, axis, [(i, (i + by) % 4) for i in range(4)])


def after(x, *others):
    return lax.optimization_barrier((x,) + others)[0]


def in_order(mine, other, index):
    return jnp.stack([jnp.where(index == 0, mine, other), jnp.where(index == 0, other, mine)])


def flip(x, axis):
    return lax.ppermute(x, axis, [(0, 1), (1, 0)])


def layer_norm_parts(residual, gain_vec, bias_vec):
    row_mean = jnp.mean(residual, -1, keepdims=True)
    centred = residual - row_mean
    variance = jnp.mean(centred * centred, -1, keepdims=True)
    inv_std = lax.rsqrt(variance + EPSILON)
    unit_rows = centred * inv_std
    return (unit_rows * gain_vec + bias_vec, unit_rows, inv_std)


def norm_back(incoming, unit_rows, inv_std, gain_vec):
    scaled = incoming * gain_vec
    return inv_std * (
        scaled
        - jnp.mean(scaled, -1, keepdims=True)
        - unit_rows * jnp.mean(scaled * unit_rows, -1, keepdims=True)
    )


def sum_to_own(part):
    seqs, slots, width = part.shape
    cells = part.reshape(seqs, 2, 2, slots // 4, width)
    ci, xi = lax.axis_index("c"), lax.axis_index("xl")
    mine = lax.dynamic_index_in_dim(cells, ci, 2, keepdims=False)
    theirs = lax.dynamic_index_in_dim(cells, 1 - ci, 2, keepdims=False)
    half = mine.astype(f32) + flip(theirs.astype(bf16), "c").astype(f32)
    mine = lax.dynamic_index_in_dim(half, xi, 1, keepdims=False)
    theirs = lax.dynamic_index_in_dim(half, 1 - xi, 1, keepdims=False)
    return mine + flip(theirs.astype(bf16), "xl").astype(f32)


def narrow_gather(x):
    return lax.all_gather(x, NARROW, axis=1, tiled=True)


def split3(x):
    hi = x.astype(bf16)
    rest = x - hi.astype(f32)
    mid = rest.astype(bf16)
    low = (rest - mid.astype(f32)).astype(bf16)
    return hi, mid, low


def key_bias(lens_ref, start, seq):
    slot = start + lax.broadcasted_iota(jnp.int32, (16, 256), 1)
    row = lax.broadcasted_iota(jnp.int32, (16, 256), 0)
    bias = jnp.where(slot < lens_ref[seq], 0.0, NEG)
    return jnp.where(row == 0, bias, jnp.where(row < 4, 1.0, 0.0)).astype(bf16)


def key_places(place_ref):
    places = []
    for back in range(NK):
        row = (place_ref[0] + NK - back) % NK
        places.append((pl.ds(pl.multiple_of(256 * row, 256), 256), place_ref[1] + 2048 * row))
    return places


def pick_tiles(lens_ref, place_ref, seq, run):
    n = jnp.int32(0)
    for tile in range(NK):
        n = n + (place_ref[1] + 2048 * tile < lens_ref[seq]).astype(jnp.int32)
    for tiles in range(1, NK + 1):
        pl.when(n == tiles)(functools.partial(run, seq, tiles))


def attend_kernel(
    lens_ref, place_ref, q_ref, kv0, kv1, kv2, kv3, out_ref, kx_ref, vx_ref, sum_ref, peak_ref
):
    row = lax.broadcasted_iota(jnp.int32, (16, 256), 0)
    one_row = jnp.where(row == 0, 1.0, 0.0).astype(bf16)
    one_rows = jnp.concatenate([one_row] * STEP, 1)
    for seq in range(2):
        for kv_ref, (here, start) in zip((kv0, kv1, kv2, kv3), key_places(place_ref)):
            extra = key_bias(lens_ref, start, seq)
            for h in range(3):
                kt = jnp.concatenate([kv_ref[seq, pl.ds(64 * h, 64), :], extra], 0)
                kx_ref[seq, h, here, :] = jnp.transpose(kt)
                vx_ref[seq, h, pl.ds(0, 64), here] = kv_ref[seq, pl.ds(192 + 64 * h, 64), :]
                vx_ref[seq, h, pl.ds(64, 16), here] = one_row

    def run(seq, tiles):
        keys = pl.ds(0, 256 * tiles)

        @pl.loop(0, NQ // STEP)
        def _(turn):
            for h in range(3):
                q = [q_ref[turn * STEP + j, seq, pl.ds(64 * h, 64), :] for j in range(STEP)]
                qx = jnp.concatenate([jnp.concatenate(q, 1), one_rows], 0)
                s = jnp.dot(kx_ref[seq, h, keys, :], qx, preferred_element_type=f32)
                peak = jnp.max(s, 0, keepdims=True)
                p = jnp.exp2(s - peak).astype(bf16)
                o = jnp.dot(vx_ref[seq, h, :, keys], p, preferred_element_type=f32)
                total = o[64:65]
                o = (o[:64] * (1.0 / total)).astype(bf16)
                for j in range(STEP):
                    here = slice(256 * j, 256 * j + 256)
                    out_ref[turn * STEP + j, seq, pl.ds(64 * h, 64), :] = o[:, here]
                    sum_ref[turn * STEP + j, seq, pl.ds(h, 1), :] = total[:, here]
                    peak_ref[turn * STEP + j, seq, pl.ds(h, 1), :] = peak[:, here]

    for seq in range(2):
        pick_tiles(lens_ref, place_ref, seq, run)
    for seq in range(2):
        for block in range(NQ):
            lse = peak_ref[block, seq, pl.ds(0, 3), :] + jnp.log2(sum_ref[block, seq, pl.ds(0, 3), :])
            rows = [part.astype(f32) for part in split3(lse)] + [jnp.zeros((7, 256), f32)]
            out_ref[block, seq, pl.ds(192, 16), :] = jnp.concatenate(rows, 0).astype(bf16)


def attend_back_kernel(
    lens_ref, place_ref, q_ref, kv0, kv1, kv2, kv3, g_ref, dq_ref, dkv0, dkv1, dkv2, dkv3,
    kx_ref, vx_ref, kt_ref, dk_ref, dv_ref,
):
    row = lax.broadcasted_iota(jnp.int32, (16, 256), 0)
    ones = jnp.where(row < 3, 1.0, 0.0).astype(bf16)
    one = jnp.ones((1, 256), f32)
    nt = (((1,), (1,)), ((), ()))
    for seq in range(2):
        for kv_ref, (here, start) in zip((kv0, kv1, kv2, kv3), key_places(place_ref)):
            extra = key_bias(lens_ref, start, seq)
            for h in range(3):
                k = kv_ref[seq, pl.ds(64 * h, 64), :]
                v = kv_ref[seq, pl.ds(192 + 64 * h, 64), :]
                kx_ref[seq, h, here, :] = jnp.transpose(jnp.concatenate([k, extra], 0))
                vx_ref[seq, h, here, :] = jnp.transpose(jnp.concatenate([v, ones], 0))
                kt_ref[seq, h, :, here] = k
    dk_ref[...] = jnp.zeros_like(dk_ref)
    dv_ref[...] = jnp.zeros_like(dv_ref)

    def run(seq, tiles):
        keys = pl.ds(0, 256 * tiles)

        @pl.loop(0, NQ)
        def _(block):
            stats = g_ref[block, seq, pl.ds(192, 32), :].astype(f32)
            for h in range(3):
                q = q_ref[block, seq, pl.ds(64 * h, 64), :]
                g = g_ref[block, seq, pl.ds(64 * h, 64), :]
                rows = [one, stats[3 * h : 3 * h + 3], jnp.zeros((12, 256), f32)]
                qx = jnp.concatenate([q, jnp.concatenate(rows, 0).astype(bf16)], 0)
                rows = [stats[16 + 3 * h : 16 + 3 * h + 3], jnp.zeros((13, 256), f32)]
                gx = jnp.concatenate([g, jnp.concatenate(rows, 0).astype(bf16)], 0)
                p = jnp.exp2(jnp.dot(kx_ref[seq, h, keys, :], qx, preferred_element_type=f32))
                d = jnp.dot(vx_ref[seq, h, keys, :], gx, preferred_element_type=f32)
                ds = (p * d).astype(bf16)
                dq = jnp.dot(kt_ref[seq, h, :, keys], ds, preferred_element_type=f32)
                dk_ref[seq, h, :, keys] += lax.dot_general(q, ds, nt, preferred_element_type=f32)
                dv_ref[seq, h, :, keys] += lax.dot_general(
                    g, p.astype(bf16), nt, preferred_element_type=f32
                )
                dq_ref[block, seq, pl.ds(64 * h, 64), :] = (dq * HEAD**-0.5).astype(bf16)

    for seq in range(2):
        pick_tiles(lens_ref, place_ref, seq, run)
    for seq in range(2):
        for dkv_ref, (here, _) in zip((dkv0, dkv1, dkv2, dkv3), key_places(place_ref)):
            for h in range(3):
                dk = dk_ref[seq, h, :, here] * (1.0 / LOG2E)
                dkv_ref[seq, pl.ds(64 * h, 64), :] = dk.astype(bf16)
                dkv_ref[seq, pl.ds(192 + 64 * h, 64), :] = dv_ref[seq, h, :, here].astype(bf16)


def unpack_kernel(where_ref, p0, p1, p2a, p2b, p3, gate_ref, up_ref, out_ref, down_ref, norm_ref):
    for back_y, part in enumerate((p0, p1, p2a, p3)):
        y = (where_ref[0] + 4 - back_y) % 4
        for back_z in range(4):
            z = (where_ref[1] + 4 - back_z) % 4
            for back_x in range(2):
                x = (where_ref[2] + back_x) % 2
                row = (y * 4 + z) * 2 + x
                block = part.at[back_z, back_x]
                if back_y == 2 and back_z >= 2:
                    block = p2b.at[back_z - 2, back_x]
                gate_ref[row] = block[0:3]
                up_ref[row] = block[3:6]
                out_ref[row] = block[6:9]
                down_ref[(z * 2 + x) * 4 + y] = block[9:12]
                norm_ref[row] = block[12]


SMEM = pl.BlockSpec(memory_space=pltpu.SMEM)
VMEM = pl.BlockSpec(memory_space=pltpu.VMEM)
PARAMS = pltpu.CompilerParams(vmem_limit_bytes=56 * 1024 * 1024)


def attend(lengths, place, q_all, kv_all):
    return pl.pallas_call(
        attend_kernel,
        out_shape=jax.ShapeDtypeStruct((NQ, 2, 208, 256), bf16),
        in_specs=[SMEM, SMEM] + [VMEM] * 5,
        out_specs=VMEM,
        scratch_shapes=[
            pltpu.VMEM((2, 3, 1024, 80), bf16),
            pltpu.VMEM((2, 3, 80, 1024), bf16),
            pltpu.VMEM((NQ, 2, 8, 256), f32),
            pltpu.VMEM((NQ, 2, 8, 256), f32),
        ],
        compiler_params=PARAMS,
        cost_estimate=pl.CostEstimate(
            flops=23_000_000_000, bytes_accessed=5_000_000, transcendentals=12_582_912
        ),
    )(lengths, place, q_all, *kv_all)


def attend_back(lengths, place, q_all, kv_all, g_all):
    return pl.pallas_call(
        attend_back_kernel,
        out_shape=(
            jax.ShapeDtypeStruct((NQ, 2, 192, 256), bf16),
        )
        + (jax.ShapeDtypeStruct((2, 384, 256), bf16),) * NK,
        in_specs=[SMEM, SMEM] + [VMEM] * 6,
        out_specs=(VMEM,) * 5,
        scratch_shapes=[
            pltpu.VMEM((2, 3, 1024, 80), bf16),
            pltpu.VMEM((2, 3, 1024, 80), bf16),
            pltpu.VMEM((2, 3, 64, 1024), bf16),
            pltpu.VMEM((2, 3, 64, 1024), f32),
            pltpu.VMEM((2, 3, 64, 1024), f32),
        ],
        compiler_params=PARAMS,
        cost_estimate=pl.CostEstimate(
            flops=46_000_000_000, bytes_accessed=8_000_000, transcendentals=12_582_912
        ),
    )(lengths, place, q_all, *kv_all, g_all)


def unpack(where, parts):
    block = jax.ShapeDtypeStruct((32, 3, 8, 768), bf16)
    *weights, norms = pl.pallas_call(
        unpack_kernel,
        out_shape=(block,) * 4 + (jax.ShapeDtypeStruct((32, 8, 768), bf16),),
        in_specs=[SMEM] + [VMEM] * 5,
        out_specs=(VMEM,) * 5,
        compiler_params=PARAMS,
        cost_estimate=pl.CostEstimate(flops=0, bytes_accessed=12_000_000, transcendentals=0),
    )(where, *parts)
    return [weight.reshape(768, 768) for weight in weights], norms


def on_device(hidden_in, lengths, w_qkv, w_out, w_gate, w_up, w_down, norm_params, cotangent):
    y_i, z_i, xh_i = (lax.axis_index(a) for a in WIDE)
    wide_i = (y_i * 4 + z_i) * 2 + xh_i
    n_i = lax.axis_index("xl") * 2 + lax.axis_index("c")
    seqs, own_slots, width = hidden_in.shape
    slots = own_slots * 4

    pair = in_order(hidden_in, flip(hidden_in, "xl"), lax.axis_index("xl"))
    tokens = in_order(pair, flip(pair, "c"), lax.axis_index("c"))
    tokens = tokens.transpose(2, 1, 0, 3, 4).reshape(seqs, slots, width)

    blocks = w_qkv.reshape(24, 3, 192).transpose(1, 0, 2)
    picks = jnp.minimum((jnp.arange(4) - 3 * n_i) % 4, 2)
    norm_row = jnp.pad(norm_params, ((0, 7), (0, 168)))
    sent = jnp.concatenate(
        [
            jnp.take(blocks, picks, axis=0),
            jnp.broadcast_to(w_out[None], (4, 24, 192)),
            w_down.reshape(4, 24, 192),
            jnp.broadcast_to(norm_row[None], (4, 8, 192)),
        ],
        axis=1,
    )
    got = exchange(sent, NARROW)
    sources = (4 * jnp.arange(3) + n_i) // 3
    qkv_mine = jnp.take(got[:, :24], sources, axis=0).transpose(1, 0, 2).reshape(24, 576)
    wqkv = gather(qkv_mine, WIDE, 32).reshape(width, 576)

    turn_pairs = [((y * 4 + n), (n * 4 + y)) for y in range(4) for n in range(4)]
    down_rows = got[:, 48:72].transpose(1, 0, 2).reshape(24, width)
    down_rows = lax.ppermute(down_rows, ("y",) + NARROW, turn_pairs)
    out_rows = got[:, 24:48].transpose(1, 0, 2).reshape(24, width)
    norm_row = jnp.pad(got[:, 72, :24].reshape(1, 96), ((0, 7), (0, width - 96)))
    packed = jnp.concatenate([w_gate, w_up, out_rows, down_rows, norm_row], axis=0)
    rows_x = jnp.stack([packed, flip(packed, "xh")])
    z_parts = [rows_x] + [along(rows_x, "z", back) for back in range(1, 4)]
    wqkv = after(wqkv, z_parts[1])

    positions = wide_i * slots + jnp.arange(slots)
    freqs = 10000.0 ** (-2.0 * jnp.arange(HEAD // 2, dtype=f32) / HEAD)
    angles = freqs[:, None] * positions.astype(f32)[None, :]
    cosine, sine = jnp.cos(angles), jnp.sin(angles)
    projected = jnp.einsum("df,std->sft", wqkv, tokens, preferred_element_type=f32)

    def rotate(block):
        halves = block.reshape(seqs, 3, 2, HEAD // 2, slots)
        first, second = halves[:, :, 0], halves[:, :, 1]
        return jnp.stack(
            [first * cosine - second * sine, second * cosine + first * sine], 2
        ).reshape(seqs, 192, slots)

    query = (rotate(projected[:, :192]) * (HEAD**-0.5 * LOG2E)).astype(bf16)
    keyval = jnp.concatenate(
        [rotate(projected[:, 192:384]), projected[:, 384:]], axis=1
    ).astype(bf16)
    q_all = gather(query, QAX, NQ)
    kv_all = [keyval] + [along(keyval, "y", back) for back in range(1, NK)]
    rows_zx = jnp.stack(after(z_parts, kv_all[1])).reshape(4, 2, 13, 8, width)
    before, behind = along(rows_zx, "y", 1), along(rows_zx, "y", 3)
    zx_parts = [rows_zx, before, along(before[:2], "y", 1), along(behind[2:], "y", 3), behind]
    place = jnp.stack([y_i, (z_i * 2 + xh_i) * slots]).astype(jnp.int32)
    parts = attend(lengths, place, q_all, kv_all)
    parts = exchange(parts, QAX).astype(f32)
    part_lse = jnp.sum(parts[:, :, 192:201].reshape(NQ, seqs, 3, 3, slots), 2)
    top = jnp.max(part_lse, 0)
    lse = top + jnp.log2(jnp.sum(jnp.exp2(part_lse - top), 0))
    shares = jnp.exp2(part_lse - lse)
    where = jnp.stack([y_i, z_i, xh_i]).astype(jnp.int32)
    (wgate, wup, wout, wdown), norms = unpack(where, zx_parts)
    norm_values = (
        norms[:, 0, :96].reshape(32, 4, 24).transpose(1, 0, 2).reshape(4, width).astype(f32)
    )
    attended = jnp.sum(
        parts[:, :, :192].reshape(NQ, seqs, 3, HEAD, slots) * shares[:, :, :, None, :], 0
    )
    attn_sent = attended.reshape(seqs, 192, slots).astype(bf16)
    attn_all = narrow_gather(attn_sent)

    projection = jnp.einsum("sft,fd->std", attn_all, wout, preferred_element_type=f32)
    normed, _, _ = layer_norm_parts(
        tokens.astype(f32) + projection, norm_values[0], norm_values[1]
    )
    normed_low = normed.astype(bf16)
    own_slice = lambda a: lax.dynamic_slice_in_dim(a, n_i * own_slots, own_slots, 1)
    own_first, unit_first, inv_first = layer_norm_parts(
        hidden_in.astype(f32) + own_slice(projection), norm_values[0], norm_values[1]
    )
    flat_low = normed_low.reshape(-1, width)
    gate_pre = jnp.dot(flat_low, wgate, preferred_element_type=f32)
    up_pre = jnp.dot(flat_low, wup, preferred_element_type=f32)
    gate_sigmoid = jax.nn.sigmoid(gate_pre)
    gate_silu = gate_pre * gate_sigmoid
    activated = (gate_silu * up_pre).astype(bf16)
    down_part = jnp.dot(activated, wdown, preferred_element_type=f32)
    down_out = sum_to_own(down_part.reshape(seqs, slots, width))
    output_rows, unit_second, inv_second = layer_norm_parts(
        own_first + down_out, norm_values[2], norm_values[3]
    )
    own_positions = wide_i * slots + n_i * own_slots + jnp.arange(own_slots)
    valid = (own_positions[None, :] < lengths[:, None]).astype(f32)[:, :, None]
    layer_out = (output_rows * valid).astype(bf16)
    grad_rows = cotangent.astype(f32) * valid
    grad_gain2 = jnp.sum(grad_rows * unit_second, (0, 1))
    grad_bias2 = jnp.sum(grad_rows, (0, 1))
    grad_second = norm_back(grad_rows, unit_second, inv_second, norm_values[2])
    down_low = narrow_gather(grad_second.astype(bf16)).reshape(-1, width)

    grad_wdown = jnp.einsum("tf,td->fd", activated, down_low, preferred_element_type=f32)
    grad_act = jnp.einsum("td,fd->tf", down_low, wdown, preferred_element_type=f32)
    silu_slope = gate_sigmoid * (1.0 + gate_pre * (1.0 - gate_sigmoid))
    grad_gate_low = (grad_act * up_pre * silu_slope).astype(bf16)
    grad_up_low = (grad_act * gate_silu).astype(bf16)
    grad_wgate = jnp.einsum("td,tf->df", flat_low, grad_gate_low, preferred_element_type=f32)
    grad_wup = jnp.einsum("td,tf->df", flat_low, grad_up_low, preferred_element_type=f32)
    first_part = jnp.einsum(
        "tf,df->td", grad_gate_low, wgate, preferred_element_type=f32
    ) + jnp.einsum("tf,df->td", grad_up_low, wup, preferred_element_type=f32)
    grad_normed = grad_second + sum_to_own(first_part.reshape(seqs, slots, width))
    grad_gain1 = jnp.sum(grad_normed * unit_first, (0, 1))
    grad_bias1 = jnp.sum(grad_normed, (0, 1))
    grad_first = norm_back(grad_normed, unit_first, inv_first, norm_values[0])
    res_low = narrow_gather(grad_first.astype(bf16))
    out_mine = lax.dynamic_slice_in_dim(wout, n_i * 192, 192, 0)
    grad_attn = jnp.einsum("fd,std->sft", out_mine, res_low, preferred_element_type=f32).astype(
        bf16
    )
    delta = jnp.sum(
        grad_attn.astype(f32).reshape(seqs, 3, HEAD, slots) * attended, 2
    )

    def three(x):
        hi = lax.reduce_precision(x, 8, 7)
        mid = lax.reduce_precision(x - hi, 8, 7)
        low = x - hi - mid
        return jnp.pad(
            jnp.stack([hi, mid, low], 2).reshape(seqs, 9, slots), ((0, 0), (0, 7), (0, 0))
        )

    sent_back = jnp.concatenate(
        [grad_attn, three(-lse).astype(bf16), three(-delta).astype(bf16)], axis=1
    )
    g_all = gather(sent_back, QAX, NQ)

    grad_norm_rows = jnp.stack([grad_gain1, grad_bias1, grad_gain2, grad_bias2])
    norm_blocks = grad_norm_rows.reshape(4, 32, 24).transpose(1, 0, 2).reshape(32, 1, 96)
    norm_blocks = jnp.pad(norm_blocks, ((0, 0), (0, 7), (0, width - 96))).astype(bf16)
    grads_packed = jnp.concatenate(
        [
            grad_wgate.astype(bf16).reshape(32, 24, width),
            grad_wup.astype(bf16).reshape(32, 24, width),
            grad_wdown.astype(bf16)
            .reshape(8, 4, 24, width)
            .transpose(1, 0, 2, 3)
            .reshape(32, 24, width),
            norm_blocks,
        ],
        axis=1,
    )
    grads_packed, g_all = lax.optimization_barrier((grads_packed, g_all))
    grads_got = exchange(grads_packed, WIDE)
    dq_parts, *dkv_parts = attend_back(lengths, place, q_all, kv_all, g_all)
    grads_got, dq_parts, dkv_parts = lax.optimization_barrier((grads_got, dq_parts, dkv_parts))
    grads_got = jnp.sum(grads_got.astype(f32), 0)
    sum_gate = grads_got[0:24]
    sum_up = grads_got[24:48]
    down_rows = lax.ppermute(grads_got[48:72].astype(bf16), ("y",) + NARROW, turn_pairs)
    norm_sums = grads_got[72, :96].reshape(4, 24)

    grad_query = jnp.sum(exchange(dq_parts, QAX).astype(f32), 0)
    grad_keyval = dkv_parts[0].astype(f32) + sum(
        along(dkv_parts[back], "y", NK - back).astype(f32) for back in range(1, NK)
    )

    def unrotate(block):
        halves = block.reshape(seqs, 3, 2, HEAD // 2, slots)
        first, second = halves[:, :, 0], halves[:, :, 1]
        return jnp.stack(
            [first * cosine + second * sine, second * cosine - first * sine], 2
        ).reshape(seqs, 192, slots)

    grad_proj = jnp.concatenate(
        [unrotate(grad_query), unrotate(grad_keyval[:, :192]), grad_keyval[:, 192:]], axis=1
    ).astype(bf16)
    grad_wqkv = jnp.einsum("std,sft->df", tokens, grad_proj, preferred_element_type=f32)
    input_part = jnp.einsum("sft,df->std", grad_proj, wqkv, preferred_element_type=f32)
    grad_input = (grad_first + sum_to_own(input_part)).astype(bf16)
    res_cols = lax.dynamic_slice_in_dim(res_low, n_i * 192, 192, 2)
    grad_wout = jnp.einsum("sft,std->fd", attn_all, res_cols, preferred_element_type=f32)
    last = jnp.concatenate([grad_wqkv.astype(bf16), grad_wout.astype(bf16)], axis=1)
    last_got = jnp.sum(exchange(last.reshape(32, 24, width), WIDE).astype(f32), 0)
    sum_out = last_got[:, 576:]
    back = last_got[:, :576].reshape(24, 3, 192).transpose(1, 0, 2)
    to = (sources[None, :] == jnp.arange(4)[:, None]).astype(f32)
    back_sent = jnp.einsum("sk,kdf->sdf", to, back).astype(bf16)
    norm_sent = jnp.pad(norm_sums[:, None, :], ((0, 0), (0, 7), (0, 168))).astype(bf16)
    down_sent = down_rows.reshape(24, 4, 192).transpose(1, 0, 2)
    back_got = exchange(jnp.concatenate([back_sent, down_sent, norm_sent], 1), NARROW).astype(f32)
    sum_down = back_got[:, 24:48].reshape(96, 192)
    sum_norms = jnp.sum(back_got[:, 48, :24], 0)[None]
    order = (3 * n_i + jnp.arange(3)) % 4
    sum_qkv = jnp.take(back_got[:, :24], order, axis=0).transpose(1, 0, 2).reshape(24, 576)
    return (layer_out, grad_input, sum_qkv, sum_out, sum_gate, sum_up, sum_down, sum_norms)


def solution(mesh):
    fine = Mesh(mesh.devices.reshape(4, 4, 2, 2, 2), AXES)
    token = P(None, WIDE + NARROW, None)
    weight = P(WIDE, NARROW)
    norm = P(NARROW, WIDE)
    return jax.shard_map(
        on_device,
        mesh=fine,
        in_specs=(token, P(), weight, weight, weight, weight, weight, norm, token),
        out_specs=(token, token, weight, weight, weight, weight, weight, norm),
        check_vma=False,
    )
```

```python
import functools
import math

import jax
import jax.numpy as jnp
from jax import lax
from jax.experimental import pallas as pl
from jax.experimental.pallas import tpu as pltpu
from jax.sharding import Mesh
from jax.sharding import PartitionSpec as P

HEADS = 12
HEAD = 64
EPSILON = 1e-05
AXES = ("y", "z", "xh", "xl", "c")
WIDE = ("y", "z", "xh")
NARROW = ("xl", "c")
QAX = ("z", "xh")
NQ = 8
NK = 4
STEP = 4
LOG2E = math.log2(math.e)
NEG = -1e30
f32 = jnp.float32
bf16 = jnp.bfloat16


def exchange(x, axes):
    return lax.all_to_all(x, axes, 0, 0, tiled=True)


def gather(x, axes, n):
    return exchange(jnp.broadcast_to(x[None], (n,) + x.shape), axes)


def along(x, axis, by):
    return lax.ppermute(x, axis, [(i, (i + by) % 4) for i in range(4)])


def after(x, *others):
    return lax.optimization_barrier((x,) + others)[0]


def round_x_z(rows):
    rows = rows.reshape(-1, 8, rows.shape[-1])
    rows = jnp.stack([rows, flip(rows, "xh")])
    return [rows] + [along(rows, "z", back) for back in range(1, 4)]


def round_y(rows):
    before, behind = along(rows, "y", 1), along(rows, "y", 3)
    return [rows, before, along(before[:2], "y", 1), along(behind[2:], "y", 3), behind]


def in_order(mine, other, index):
    return jnp.stack([jnp.where(index == 0, mine, other), jnp.where(index == 0, other, mine)])


def flip(x, axis):
    return lax.ppermute(x, axis, [(0, 1), (1, 0)])


def layer_norm_parts(residual, gain_vec, bias_vec):
    row_mean = jnp.mean(residual, -1, keepdims=True)
    centred = residual - row_mean
    variance = jnp.mean(centred * centred, -1, keepdims=True)
    inv_std = lax.rsqrt(variance + EPSILON)
    unit_rows = centred * inv_std
    return (unit_rows * gain_vec + bias_vec, unit_rows, inv_std)


def norm_back(incoming, unit_rows, inv_std, gain_vec):
    scaled = incoming * gain_vec
    return inv_std * (
        scaled
        - jnp.mean(scaled, -1, keepdims=True)
        - unit_rows * jnp.mean(scaled * unit_rows, -1, keepdims=True)
    )


def sum_to_own(part):
    seqs, slots, width = part.shape
    cells = part.reshape(seqs, 2, 2, slots // 4, width)
    ci, xi = lax.axis_index("c"), lax.axis_index("xl")
    mine = lax.dynamic_index_in_dim(cells, ci, 2, keepdims=False)
    theirs = lax.dynamic_index_in_dim(cells, 1 - ci, 2, keepdims=False)
    half = mine.astype(f32) + flip(theirs.astype(bf16), "c").astype(f32)
    mine = lax.dynamic_index_in_dim(half, xi, 1, keepdims=False)
    theirs = lax.dynamic_index_in_dim(half, 1 - xi, 1, keepdims=False)
    return mine + flip(theirs.astype(bf16), "xl").astype(f32)


def narrow_gather(x):
    return lax.all_gather(x, NARROW, axis=1, tiled=True)


def split3(x):
    hi = x.astype(bf16)
    rest = x - hi.astype(f32)
    mid = rest.astype(bf16)
    low = (rest - mid.astype(f32)).astype(bf16)
    return hi, mid, low


def key_bias(lens_ref, start, seq):
    slot = start + lax.broadcasted_iota(jnp.int32, (16, 256), 1)
    row = lax.broadcasted_iota(jnp.int32, (16, 256), 0)
    bias = jnp.where(slot < lens_ref[seq], 0.0, NEG)
    return jnp.where(row == 0, bias, jnp.where(row < 4, 1.0, 0.0)).astype(bf16)


def key_places(place_ref):
    places = []
    for back in range(NK):
        row = (place_ref[0] + NK - back) % NK
        places.append((pl.ds(pl.multiple_of(256 * row, 256), 256), place_ref[1] + 2048 * row))
    return places


def pick_tiles(lens_ref, place_ref, seq, run):
    n = jnp.int32(0)
    for tile in range(NK):
        n = n + (place_ref[1] + 2048 * tile < lens_ref[seq]).astype(jnp.int32)
    for tiles in range(1, NK + 1):
        pl.when(n == tiles)(functools.partial(run, seq, tiles))


def attend_kernel(
    lens_ref, place_ref, q_ref, kv0, kv1, kv2, kv3, out_ref, kx_ref, vx_ref, sum_ref, peak_ref
):
    row = lax.broadcasted_iota(jnp.int32, (16, 256), 0)
    one_row = jnp.where(row == 0, 1.0, 0.0).astype(bf16)
    one_rows = jnp.concatenate([one_row] * STEP, 1)
    for seq in range(2):
        for kv_ref, (here, start) in zip((kv0, kv1, kv2, kv3), key_places(place_ref)):
            extra = key_bias(lens_ref, start, seq)
            for h in range(3):
                kt = jnp.concatenate([kv_ref[seq, pl.ds(64 * h, 64), :], extra], 0)
                kx_ref[seq, h, here, :] = jnp.transpose(kt)
                vx_ref[seq, h, pl.ds(0, 64), here] = kv_ref[seq, pl.ds(192 + 64 * h, 64), :]
                vx_ref[seq, h, pl.ds(64, 16), here] = one_row

    def run(seq, tiles, bounded):
        keys = pl.ds(0, 256 * tiles)

        @pl.loop(0, NQ // STEP)
        def _(turn):
            for h in range(3):
                q = [q_ref[turn * STEP + j, seq, pl.ds(64 * h, 64), :] for j in range(STEP)]
                qx = jnp.concatenate([jnp.concatenate(q, 1), one_rows], 0)
                s = jnp.dot(kx_ref[seq, h, keys, :], qx, preferred_element_type=f32)
                if bounded:
                    peak = jnp.zeros((1, 256 * STEP), f32)
                    p = jnp.exp2(s).astype(bf16)
                else:
                    peak = jnp.max(s, 0, keepdims=True)
                    p = jnp.exp2(s - peak).astype(bf16)
                o = jnp.dot(vx_ref[seq, h, :, keys], p, preferred_element_type=f32)
                total = o[64:65]
                o = (o[:64] * (1.0 / total)).astype(bf16)
                for j in range(STEP):
                    here = slice(256 * j, 256 * j + 256)
                    out_ref[turn * STEP + j, seq, pl.ds(64 * h, 64), :] = o[:, here]
                    sum_ref[turn * STEP + j, seq, pl.ds(h, 1), :] = total[:, here]
                    peak_ref[turn * STEP + j, seq, pl.ds(h, 1), :] = peak[:, here]

    top_key = jnp.zeros((1, 256), f32)
    for kv_ref in (kv0, kv1, kv2, kv3):
        for seq in range(2):
            for h in range(3):
                k = kv_ref[seq, pl.ds(64 * h, 64), :].astype(f32)
                top_key = jnp.maximum(top_key, jnp.sum(k * k, 0, keepdims=True))

    def widest(block, top):
        for seq in range(2):
            for h in range(3):
                q = q_ref[block, seq, pl.ds(64 * h, 64), :].astype(f32)
                top = jnp.maximum(top, jnp.sum(q * q, 0, keepdims=True))
        return top

    top_query = lax.fori_loop(0, NQ, widest, jnp.zeros((1, 256), f32))
    bounded = jnp.max(top_key) * jnp.max(top_query) < 100.0**2

    @pl.when(bounded)
    def _():
        for seq in range(2):
            pick_tiles(lens_ref, place_ref, seq, functools.partial(run, bounded=True))

    @pl.when(jnp.logical_not(bounded))
    def _():
        for seq in range(2):
            run(seq, NK, False)

    for seq in range(2):
        for block in range(NQ):
            lse = peak_ref[block, seq, pl.ds(0, 3), :] + jnp.log2(sum_ref[block, seq, pl.ds(0, 3), :])
            rows = [part.astype(f32) for part in split3(lse)] + [jnp.zeros((7, 256), f32)]
            out_ref[block, seq, pl.ds(192, 16), :] = jnp.concatenate(rows, 0).astype(bf16)


def attend_back_kernel(
    lens_ref, place_ref, q_ref, kv0, kv1, kv2, kv3, g_ref, dq_ref, dkv0, dkv1, dkv2, dkv3,
    kx_ref, vx_ref, kt_ref, dk_ref, dv_ref,
):
    row = lax.broadcasted_iota(jnp.int32, (16, 256), 0)
    ones = jnp.where(row < 3, 1.0, 0.0).astype(bf16)
    one = jnp.ones((1, 256), f32)
    nt = (((1,), (1,)), ((), ()))
    for seq in range(2):
        for kv_ref, (here, start) in zip((kv0, kv1, kv2, kv3), key_places(place_ref)):
            extra = key_bias(lens_ref, start, seq)
            for h in range(3):
                k = kv_ref[seq, pl.ds(64 * h, 64), :]
                v = kv_ref[seq, pl.ds(192 + 64 * h, 64), :]
                kx_ref[seq, h, here, :] = jnp.transpose(jnp.concatenate([k, extra], 0))
                vx_ref[seq, h, here, :] = jnp.transpose(jnp.concatenate([v, ones], 0))
                kt_ref[seq, h, :, here] = k
    dk_ref[...] = jnp.zeros_like(dk_ref)
    dv_ref[...] = jnp.zeros_like(dv_ref)

    def run(seq, tiles):
        keys = pl.ds(0, 256 * tiles)

        @pl.loop(0, NQ)
        def _(block):
            stats = g_ref[block, seq, pl.ds(192, 32), :].astype(f32)
            for h in range(3):
                q = q_ref[block, seq, pl.ds(64 * h, 64), :]
                g = g_ref[block, seq, pl.ds(64 * h, 64), :]
                rows = [one, stats[3 * h : 3 * h + 3], jnp.zeros((12, 256), f32)]
                qx = jnp.concatenate([q, jnp.concatenate(rows, 0).astype(bf16)], 0)
                rows = [stats[16 + 3 * h : 16 + 3 * h + 3], jnp.zeros((13, 256), f32)]
                gx = jnp.concatenate([g, jnp.concatenate(rows, 0).astype(bf16)], 0)
                p = jnp.exp2(jnp.dot(kx_ref[seq, h, keys, :], qx, preferred_element_type=f32))
                d = jnp.dot(vx_ref[seq, h, keys, :], gx, preferred_element_type=f32)
                ds = (p * d).astype(bf16)
                dq = jnp.dot(kt_ref[seq, h, :, keys], ds, preferred_element_type=f32)
                dk_ref[seq, h, :, keys] += lax.dot_general(q, ds, nt, preferred_element_type=f32)
                dv_ref[seq, h, :, keys] += lax.dot_general(
                    g, p.astype(bf16), nt, preferred_element_type=f32
                )
                dq_ref[block, seq, pl.ds(64 * h, 64), :] = (dq * HEAD**-0.5).astype(bf16)

    for seq in range(2):
        pick_tiles(lens_ref, place_ref, seq, run)
    for seq in range(2):
        for dkv_ref, (here, _) in zip((dkv0, dkv1, dkv2, dkv3), key_places(place_ref)):
            for h in range(3):
                dk = dk_ref[seq, h, :, here] * (1.0 / LOG2E)
                dkv_ref[seq, pl.ds(64 * h, 64), :] = dk.astype(bf16)
                dkv_ref[seq, pl.ds(192 + 64 * h, 64), :] = dv_ref[seq, h, :, here].astype(bf16)


def unpack_kernel(where_ref, *refs):
    first, second = refs[:5], refs[5:10]
    gate_ref, up_ref, out_ref, down_ref, norm_ref = refs[10:]
    for back_y in range(4):
        y = (where_ref[0] + 4 - back_y) % 4
        for back_z in range(4):
            z = (where_ref[1] + 4 - back_z) % 4
            index, inner = ((0, 1, 2, 4)[back_y], back_z)
            if back_y == 2 and back_z >= 2:
                index, inner = 3, back_z - 2
            for back_x in range(2):
                x = (where_ref[2] + back_x) % 2
                row = (y * 4 + z) * 2 + x
                block = first[index].at[inner, back_x]
                gate_ref[row] = block[0:3]
                up_ref[row] = block[3:6]
                block = second[index].at[inner, back_x]
                out_ref[row] = block[0:3]
                down_ref[(z * 2 + x) * 4 + y] = block[3:6]
                norm_ref[row] = block[6]


SMEM = pl.BlockSpec(memory_space=pltpu.SMEM)
VMEM = pl.BlockSpec(memory_space=pltpu.VMEM)
PARAMS = pltpu.CompilerParams(vmem_limit_bytes=56 * 1024 * 1024)


def attend(lengths, place, q_all, kv_all):
    return pl.pallas_call(
        attend_kernel,
        out_shape=jax.ShapeDtypeStruct((NQ, 2, 208, 256), bf16),
        in_specs=[SMEM, SMEM] + [VMEM] * 5,
        out_specs=VMEM,
        scratch_shapes=[
            pltpu.VMEM((2, 3, 1024, 80), bf16),
            pltpu.VMEM((2, 3, 80, 1024), bf16),
            pltpu.VMEM((NQ, 2, 8, 256), f32),
            pltpu.VMEM((NQ, 2, 8, 256), f32),
        ],
        compiler_params=PARAMS,
        cost_estimate=pl.CostEstimate(
            flops=23_000_000_000, bytes_accessed=5_000_000, transcendentals=12_582_912
        ),
    )(lengths, place, q_all, *kv_all)


def attend_back(lengths, place, q_all, kv_all, g_all):
    return pl.pallas_call(
        attend_back_kernel,
        out_shape=(
            jax.ShapeDtypeStruct((NQ, 2, 192, 256), bf16),
        )
        + (jax.ShapeDtypeStruct((2, 384, 256), bf16),) * NK,
        in_specs=[SMEM, SMEM] + [VMEM] * 6,
        out_specs=(VMEM,) * 5,
        scratch_shapes=[
            pltpu.VMEM((2, 3, 1024, 80), bf16),
            pltpu.VMEM((2, 3, 1024, 80), bf16),
            pltpu.VMEM((2, 3, 64, 1024), bf16),
            pltpu.VMEM((2, 3, 64, 1024), f32),
            pltpu.VMEM((2, 3, 64, 1024), f32),
        ],
        compiler_params=PARAMS,
        cost_estimate=pl.CostEstimate(
            flops=46_000_000_000, bytes_accessed=8_000_000, transcendentals=12_582_912
        ),
    )(lengths, place, q_all, *kv_all, g_all)


def unpack(where, parts):
    block = jax.ShapeDtypeStruct((32, 3, 8, 768), bf16)
    *weights, norms = pl.pallas_call(
        unpack_kernel,
        out_shape=(block,) * 4 + (jax.ShapeDtypeStruct((32, 8, 768), bf16),),
        in_specs=[SMEM] + [VMEM] * 10,
        out_specs=(VMEM,) * 5,
        compiler_params=PARAMS,
        cost_estimate=pl.CostEstimate(flops=0, bytes_accessed=12_000_000, transcendentals=0),
    )(where, *parts)
    return [weight.reshape(768, 768) for weight in weights], norms


def on_device(hidden_in, lengths, w_qkv, w_out, w_gate, w_up, w_down, norm_params, cotangent):
    y_i, z_i, xh_i = (lax.axis_index(a) for a in WIDE)
    wide_i = (y_i * 4 + z_i) * 2 + xh_i
    n_i = lax.axis_index("xl") * 2 + lax.axis_index("c")
    seqs, own_slots, width = hidden_in.shape
    slots = own_slots * 4

    pair = in_order(hidden_in, flip(hidden_in, "xl"), lax.axis_index("xl"))
    tokens = in_order(pair, flip(pair, "c"), lax.axis_index("c"))
    tokens = tokens.transpose(2, 1, 0, 3, 4).reshape(seqs, slots, width)

    first_z = round_x_z(jnp.concatenate([w_gate, w_up]))
    sent = []
    for to in range(4):
        pick = (to - 3 * n_i) % 4
        block = jnp.where(
            pick == 0, w_qkv[:, :192], jnp.where(pick == 1, w_qkv[:, 192:384], w_qkv[:, 384:])
        )
        norm_row = jnp.pad(norm_params, ((0, 7), (0, 168)))
        sent.append(jnp.concatenate([block, w_out, w_down[24 * to : 24 * to + 24], norm_row]))
    got = exchange(jnp.stack(sent), NARROW)
    sources = (4 * jnp.arange(3) + n_i) // 3
    qkv_mine = jnp.take(got[:, :24], sources, axis=0).transpose(1, 0, 2).reshape(24, 576)
    wqkv = gather(qkv_mine, WIDE, 32).reshape(width, 576)

    turn_pairs = [((y * 4 + n), (n * 4 + y)) for y in range(4) for n in range(4)]
    down_rows = got[:, 48:72].transpose(1, 0, 2).reshape(24, width)
    down_rows = lax.ppermute(down_rows, ("y",) + NARROW, turn_pairs)
    out_rows = got[:, 24:48].transpose(1, 0, 2).reshape(24, width)
    norm_row = jnp.pad(got[:, 72, :24].reshape(1, 96), ((0, 7), (0, width - 96)))
    second_z = round_x_z(jnp.concatenate([out_rows, down_rows, norm_row]))
    first_rows = jnp.stack(first_z)
    first_parts = round_y(first_rows)
    wqkv = after(wqkv, first_rows, second_z[0])

    positions = wide_i * slots + jnp.arange(slots)
    freqs = 10000.0 ** (-2.0 * jnp.arange(HEAD // 2, dtype=f32) / HEAD)
    angles = freqs[:, None] * positions.astype(f32)[None, :]
    cosine, sine = jnp.cos(angles), jnp.sin(angles)
    projected = jnp.einsum("df,std->sft", wqkv, tokens, preferred_element_type=f32)

    def rotate(block):
        halves = block.reshape(seqs, 3, 2, HEAD // 2, slots)
        first, second = halves[:, :, 0], halves[:, :, 1]
        return jnp.stack(
            [first * cosine - second * sine, second * cosine + first * sine], 2
        ).reshape(seqs, 192, slots)

    query = (rotate(projected[:, :192]) * (HEAD**-0.5 * LOG2E)).astype(bf16)
    keyval = jnp.concatenate(
        [rotate(projected[:, 192:384]), projected[:, 384:]], axis=1
    ).astype(bf16)
    q_all = gather(query, QAX, NQ)
    kv_all = [keyval] + [along(keyval, "y", back) for back in range(1, NK)]
    second_parts = round_y(jnp.stack(after(second_z, kv_all[1])))
    place = jnp.stack([y_i, (z_i * 2 + xh_i) * slots]).astype(jnp.int32)
    place = after(place, first_parts[1], first_parts[4])
    parts = attend(lengths, place, q_all, kv_all)
    parts = after(parts, *first_parts, second_parts[1], second_parts[4])
    parts = exchange(parts, QAX).astype(f32)
    part_lse = jnp.sum(parts[:, :, 192:201].reshape(NQ, seqs, 3, 3, slots), 2)
    top = jnp.max(part_lse, 0)
    lse = top + jnp.log2(jnp.sum(jnp.exp2(part_lse - top), 0))
    shares = jnp.exp2(part_lse - lse)
    where = jnp.stack([y_i, z_i, xh_i]).astype(jnp.int32)
    (wgate, wup, wout, wdown), norms = unpack(where, first_parts + second_parts)
    norm_values = (
        norms[:, 0, :96].reshape(32, 4, 24).transpose(1, 0, 2).reshape(4, width).astype(f32)
    )
    attended = jnp.sum(
        parts[:, :, :192].reshape(NQ, seqs, 3, HEAD, slots) * shares[:, :, :, None, :], 0
    )
    attn_sent = attended.reshape(seqs, 192, slots).astype(bf16)
    attn_all = narrow_gather(attn_sent)

    projection = jnp.einsum("sft,fd->std", attn_all, wout, preferred_element_type=f32)
    normed, _, _ = layer_norm_parts(
        tokens.astype(f32) + projection, norm_values[0], norm_values[1]
    )
    normed_low = normed.astype(bf16)
    own_slice = lambda a: lax.dynamic_slice_in_dim(a, n_i * own_slots, own_slots, 1)
    own_first, unit_first, inv_first = layer_norm_parts(
        hidden_in.astype(f32) + own_slice(projection), norm_values[0], norm_values[1]
    )
    flat_low = normed_low.reshape(-1, width)
    gate_pre = jnp.dot(flat_low, wgate, preferred_element_type=f32)
    up_pre = jnp.dot(flat_low, wup, preferred_element_type=f32)
    gate_sigmoid = jax.nn.sigmoid(gate_pre)
    gate_silu = gate_pre * gate_sigmoid
    activated = (gate_silu * up_pre).astype(bf16)
    down_part = jnp.dot(activated, wdown, preferred_element_type=f32)
    down_out = sum_to_own(down_part.reshape(seqs, slots, width))
    output_rows, unit_second, inv_second = layer_norm_parts(
        own_first + down_out, norm_values[2], norm_values[3]
    )
    own_positions = wide_i * slots + n_i * own_slots + jnp.arange(own_slots)
    valid = (own_positions[None, :] < lengths[:, None]).astype(f32)[:, :, None]
    layer_out = (output_rows * valid).astype(bf16)
    grad_rows = cotangent.astype(f32) * valid
    grad_gain2 = jnp.sum(grad_rows * unit_second, (0, 1))
    grad_bias2 = jnp.sum(grad_rows, (0, 1))
    grad_second = norm_back(grad_rows, unit_second, inv_second, norm_values[2])
    down_low = narrow_gather(grad_second.astype(bf16)).reshape(-1, width)

    grad_wdown = jnp.einsum("tf,td->fd", activated, down_low, preferred_element_type=f32)
    grad_act = jnp.einsum("td,fd->tf", down_low, wdown, preferred_element_type=f32)
    silu_slope = gate_sigmoid * (1.0 + gate_pre * (1.0 - gate_sigmoid))
    grad_gate_low = (grad_act * up_pre * silu_slope).astype(bf16)
    grad_up_low = (grad_act * gate_silu).astype(bf16)
    grad_wgate = jnp.einsum("td,tf->df", flat_low, grad_gate_low, preferred_element_type=f32)
    grad_wup = jnp.einsum("td,tf->df", flat_low, grad_up_low, preferred_element_type=f32)
    first_part = jnp.einsum(
        "tf,df->td", grad_gate_low, wgate, preferred_element_type=f32
    ) + jnp.einsum("tf,df->td", grad_up_low, wup, preferred_element_type=f32)
    grad_normed = grad_second + sum_to_own(first_part.reshape(seqs, slots, width))
    grad_gain1 = jnp.sum(grad_normed * unit_first, (0, 1))
    grad_bias1 = jnp.sum(grad_normed, (0, 1))
    grad_first = norm_back(grad_normed, unit_first, inv_first, norm_values[0])
    res_low = narrow_gather(grad_first.astype(bf16))
    out_mine = lax.dynamic_slice_in_dim(wout, n_i * 192, 192, 0)
    grad_attn = jnp.einsum("fd,std->sft", out_mine, res_low, preferred_element_type=f32).astype(
        bf16
    )
    delta = jnp.sum(
        grad_attn.astype(f32).reshape(seqs, 3, HEAD, slots) * attended, 2
    )

    def three(x):
        hi = lax.reduce_precision(x, 8, 7)
        mid = lax.reduce_precision(x - hi, 8, 7)
        low = x - hi - mid
        return jnp.pad(
            jnp.stack([hi, mid, low], 2).reshape(seqs, 9, slots), ((0, 0), (0, 7), (0, 0))
        )

    sent_back = jnp.concatenate(
        [grad_attn, three(-lse).astype(bf16), three(-delta).astype(bf16)], axis=1
    )
    g_all = gather(sent_back, QAX, NQ)

    grad_norm_rows = jnp.stack([grad_gain1, grad_bias1, grad_gain2, grad_bias2])
    norm_blocks = grad_norm_rows.reshape(4, 32, 24).transpose(1, 0, 2).reshape(32, 1, 96)
    norm_blocks = jnp.pad(norm_blocks, ((0, 0), (0, 7), (0, width - 96))).astype(bf16)
    grads_packed = jnp.concatenate(
        [
            grad_wgate.astype(bf16).reshape(32, 24, width),
            grad_wup.astype(bf16).reshape(32, 24, width),
            grad_wdown.astype(bf16)
            .reshape(8, 4, 24, width)
            .transpose(1, 0, 2, 3)
            .reshape(32, 24, width),
            norm_blocks,
        ],
        axis=1,
    )
    grads_packed, g_all = lax.optimization_barrier((grads_packed, g_all))
    grads_got = exchange(grads_packed, WIDE)
    dq_parts, *dkv_parts = attend_back(lengths, place, q_all, kv_all, g_all)
    grads_got, dq_parts, dkv_parts = lax.optimization_barrier((grads_got, dq_parts, dkv_parts))
    grads_got = jnp.sum(grads_got.astype(f32), 0)
    sum_gate = grads_got[0:24]
    sum_up = grads_got[24:48]
    down_rows = lax.ppermute(grads_got[48:72].astype(bf16), ("y",) + NARROW, turn_pairs)
    norm_sums = grads_got[72, :96].reshape(4, 24)

    grad_query = jnp.sum(exchange(dq_parts, QAX).astype(f32), 0)
    grad_keyval = dkv_parts[0].astype(f32) + sum(
        along(dkv_parts[back], "y", NK - back).astype(f32) for back in range(1, NK)
    )

    def unrotate(block):
        halves = block.reshape(seqs, 3, 2, HEAD // 2, slots)
        first, second = halves[:, :, 0], halves[:, :, 1]
        return jnp.stack(
            [first * cosine + second * sine, second * cosine - first * sine], 2
        ).reshape(seqs, 192, slots)

    grad_proj = jnp.concatenate(
        [unrotate(grad_query), unrotate(grad_keyval[:, :192]), grad_keyval[:, 192:]], axis=1
    ).astype(bf16)
    grad_wqkv = jnp.einsum("std,sft->df", tokens, grad_proj, preferred_element_type=f32)
    input_part = jnp.einsum("sft,df->std", grad_proj, wqkv, preferred_element_type=f32)
    grad_input = (grad_first + sum_to_own(input_part)).astype(bf16)
    res_cols = lax.dynamic_slice_in_dim(res_low, n_i * 192, 192, 2)
    grad_wout = jnp.einsum("sft,std->fd", attn_all, res_cols, preferred_element_type=f32)
    last = jnp.concatenate([grad_wqkv.astype(bf16), grad_wout.astype(bf16)], axis=1)
    last_got = jnp.sum(exchange(last.reshape(32, 24, width), WIDE).astype(f32), 0)
    sum_out = last_got[:, 576:]
    back = last_got[:, :576].reshape(24, 3, 192).transpose(1, 0, 2)
    to = (sources[None, :] == jnp.arange(4)[:, None]).astype(f32)
    back_sent = jnp.einsum("sk,kdf->sdf", to, back).astype(bf16)
    norm_sent = jnp.pad(norm_sums[:, None, :], ((0, 0), (0, 7), (0, 168))).astype(bf16)
    down_sent = down_rows.reshape(24, 4, 192).transpose(1, 0, 2)
    back_got = exchange(jnp.concatenate([back_sent, down_sent, norm_sent], 1), NARROW).astype(f32)
    sum_down = back_got[:, 24:48].reshape(96, 192)
    sum_norms = jnp.sum(back_got[:, 48, :24], 0)[None]
    order = (3 * n_i + jnp.arange(3)) % 4
    sum_qkv = jnp.take(back_got[:, :24], order, axis=0).transpose(1, 0, 2).reshape(24, 576)
    return (layer_out, grad_input, sum_qkv, sum_out, sum_gate, sum_up, sum_down, sum_norms)


def solution(mesh):
    fine = Mesh(mesh.devices.reshape(4, 4, 2, 2, 2), AXES)
    token = P(None, WIDE + NARROW, None)
    weight = P(WIDE, NARROW)
    norm = P(NARROW, WIDE)
    return jax.shard_map(
        on_device,
        mesh=fine,
        in_specs=(token, P(), weight, weight, weight, weight, weight, norm, token),
        out_specs=(token, token, weight, weight, weight, weight, weight, norm),
        check_vma=False,
    )
```

```python
import functools
import math

import jax
import jax.numpy as jnp
from jax import lax
from jax.experimental import pallas as pl
from jax.experimental.pallas import tpu as pltpu
from jax.sharding import Mesh
from jax.sharding import PartitionSpec as P

HEADS = 12
HEAD = 64
EPSILON = 1e-05
AXES = ("y", "z", "xh", "xl", "c")
WIDE = ("y", "z", "xh")
NARROW = ("xl", "c")
QAX = ("z", "xh")
NQ = 8
NK = 4
STEP = 4
LOG2E = math.log2(math.e)
NEG = -1e30
f32 = jnp.float32
bf16 = jnp.bfloat16


def exchange(x, axes):
    return lax.all_to_all(x, axes, 0, 0, tiled=True)


def gather(x, axes, n):
    return exchange(jnp.broadcast_to(x[None], (n,) + x.shape), axes)


def along(x, axis, by):
    return lax.ppermute(x, axis, [(i, (i + by) % 4) for i in range(4)])


def after(x, *others):
    return lax.optimization_barrier((x,) + others)[0]


def round_x_z(rows):
    rows = rows.reshape(-1, 8, rows.shape[-1])
    rows = jnp.stack([rows, flip(rows, "xh")])
    return [rows] + [along(rows, "z", back) for back in range(1, 4)]


def round_y(rows):
    before, behind = along(rows, "y", 1), along(rows, "y", 3)
    return [rows, before, along(before[:2], "y", 1), along(behind[2:], "y", 3), behind]


def in_order(mine, other, index):
    return jnp.stack([jnp.where(index == 0, mine, other), jnp.where(index == 0, other, mine)])


def flip(x, axis):
    return lax.ppermute(x, axis, [(0, 1), (1, 0)])


def layer_norm_parts(residual, gain_vec, bias_vec):
    row_mean = jnp.mean(residual, -1, keepdims=True)
    centred = residual - row_mean
    variance = jnp.mean(centred * centred, -1, keepdims=True)
    inv_std = lax.rsqrt(variance + EPSILON)
    unit_rows = centred * inv_std
    return (unit_rows * gain_vec + bias_vec, unit_rows, inv_std)


def norm_back(incoming, unit_rows, inv_std, gain_vec):
    scaled = incoming * gain_vec
    return inv_std * (
        scaled
        - jnp.mean(scaled, -1, keepdims=True)
        - unit_rows * jnp.mean(scaled * unit_rows, -1, keepdims=True)
    )


def sum_to_own(part):
    seqs, slots, width = part.shape
    cells = part.reshape(seqs, 2, 2, slots // 4, width)
    ci, xi = lax.axis_index("c"), lax.axis_index("xl")
    mine = lax.dynamic_index_in_dim(cells, ci, 2, keepdims=False)
    theirs = lax.dynamic_index_in_dim(cells, 1 - ci, 2, keepdims=False)
    half = mine.astype(f32) + flip(theirs.astype(bf16), "c").astype(f32)
    mine = lax.dynamic_index_in_dim(half, xi, 1, keepdims=False)
    theirs = lax.dynamic_index_in_dim(half, 1 - xi, 1, keepdims=False)
    return mine + flip(theirs.astype(bf16), "xl").astype(f32)


def narrow_gather(x):
    return lax.all_gather(x, NARROW, axis=1, tiled=True)


def split3(x):
    hi = x.astype(bf16)
    rest = x - hi.astype(f32)
    mid = rest.astype(bf16)
    low = (rest - mid.astype(f32)).astype(bf16)
    return hi, mid, low


def key_bias(lens_ref, start, seq):
    slot = start + lax.broadcasted_iota(jnp.int32, (16, 256), 1)
    row = lax.broadcasted_iota(jnp.int32, (16, 256), 0)
    bias = jnp.where(slot < lens_ref[seq], 0.0, NEG)
    return jnp.where(row == 0, bias, jnp.where(row < 4, 1.0, 0.0)).astype(bf16)


def key_places(place_ref):
    places = []
    for back in range(NK):
        row = (place_ref[0] + NK - back) % NK
        places.append((pl.ds(pl.multiple_of(256 * row, 256), 256), place_ref[1] + 2048 * row))
    return places


def pick_tiles(lens_ref, place_ref, seq, run):
    n = jnp.int32(0)
    for tile in range(NK):
        n = n + (place_ref[1] + 2048 * tile < lens_ref[seq]).astype(jnp.int32)
    for tiles in range(1, NK + 1):
        pl.when(n == tiles)(functools.partial(run, seq, tiles))


def attend_kernel(
    lens_ref, place_ref, q_ref, kv0, kv1, kv2, kv3, out_ref, kx_ref, vx_ref, sum_ref, peak_ref
):
    row = lax.broadcasted_iota(jnp.int32, (16, 256), 0)
    one_row = jnp.where(row == 0, 1.0, 0.0).astype(bf16)
    one_rows = jnp.concatenate([one_row] * STEP, 1)
    for seq in range(2):
        for kv_ref, (here, start) in zip((kv0, kv1, kv2, kv3), key_places(place_ref)):
            extra = key_bias(lens_ref, start, seq)
            for h in range(3):
                kt = jnp.concatenate([kv_ref[seq, pl.ds(64 * h, 64), :], extra], 0)
                kx_ref[seq, h, here, :] = jnp.transpose(kt)
                vx_ref[seq, h, pl.ds(0, 64), here] = kv_ref[seq, pl.ds(192 + 64 * h, 64), :]
                vx_ref[seq, h, pl.ds(64, 16), here] = one_row

    def run(seq, tiles, bounded):
        keys = pl.ds(0, 256 * tiles)

        @pl.loop(0, NQ // STEP)
        def _(turn):
            for h in range(3):
                q = [q_ref[turn * STEP + j, seq, pl.ds(64 * h, 64), :] for j in range(STEP)]
                qx = jnp.concatenate([jnp.concatenate(q, 1), one_rows], 0)
                s = jnp.dot(kx_ref[seq, h, keys, :], qx, preferred_element_type=f32)
                if bounded:
                    peak = jnp.zeros((1, 256 * STEP), f32)
                    p = jnp.exp2(s).astype(bf16)
                else:
                    peak = jnp.max(s, 0, keepdims=True)
                    p = jnp.exp2(s - peak).astype(bf16)
                o = jnp.dot(vx_ref[seq, h, :, keys], p, preferred_element_type=f32)
                total = o[64:65]
                o = (o[:64] * (1.0 / total)).astype(bf16)
                for j in range(STEP):
                    here = slice(256 * j, 256 * j + 256)
                    out_ref[turn * STEP + j, seq, pl.ds(64 * h, 64), :] = o[:, here]
                    sum_ref[turn * STEP + j, seq, pl.ds(h, 1), :] = total[:, here]
                    peak_ref[turn * STEP + j, seq, pl.ds(h, 1), :] = peak[:, here]

    top_key = jnp.zeros((1, 256), f32)
    for kv_ref in (kv0, kv1, kv2, kv3):
        for seq in range(2):
            for h in range(3):
                k = kv_ref[seq, pl.ds(64 * h, 64), :].astype(f32)
                top_key = jnp.maximum(top_key, jnp.sum(k * k, 0, keepdims=True))

    def widest(block, top):
        for seq in range(2):
            for h in range(3):
                q = q_ref[block, seq, pl.ds(64 * h, 64), :].astype(f32)
                top = jnp.maximum(top, jnp.sum(q * q, 0, keepdims=True))
        return top

    top_query = lax.fori_loop(0, NQ, widest, jnp.zeros((1, 256), f32))
    bounded = jnp.max(top_key) * jnp.max(top_query) < 100.0**2

    @pl.when(bounded)
    def _():
        for seq in range(2):
            pick_tiles(lens_ref, place_ref, seq, functools.partial(run, bounded=True))

    @pl.when(jnp.logical_not(bounded))
    def _():
        for seq in range(2):
            run(seq, NK, False)

    for seq in range(2):
        for block in range(NQ):
            lse = peak_ref[block, seq, pl.ds(0, 3), :] + jnp.log2(sum_ref[block, seq, pl.ds(0, 3), :])
            rows = [part.astype(f32) for part in split3(lse)] + [jnp.zeros((7, 256), f32)]
            out_ref[block, seq, pl.ds(192, 16), :] = jnp.concatenate(rows, 0).astype(bf16)


def attend_back_kernel(
    lens_ref, place_ref, q_ref, kv0, kv1, kv2, kv3, g_ref, dq_ref, dkv0, dkv1, dkv2, dkv3,
    kx_ref, vx_ref, kt_ref, dk_ref, dv_ref,
):
    row = lax.broadcasted_iota(jnp.int32, (16, 256), 0)
    ones = jnp.where(row < 3, 1.0, 0.0).astype(bf16)
    one = jnp.ones((1, 256), f32)
    nt = (((1,), (1,)), ((), ()))
    for seq in range(2):
        for kv_ref, (here, start) in zip((kv0, kv1, kv2, kv3), key_places(place_ref)):
            extra = key_bias(lens_ref, start, seq)
            for h in range(3):
                k = kv_ref[seq, pl.ds(64 * h, 64), :]
                v = kv_ref[seq, pl.ds(192 + 64 * h, 64), :]
                kx_ref[seq, h, here, :] = jnp.transpose(jnp.concatenate([k, extra], 0))
                vx_ref[seq, h, here, :] = jnp.transpose(jnp.concatenate([v, ones], 0))
                kt_ref[seq, h, :, here] = k
    dk_ref[...] = jnp.zeros_like(dk_ref)
    dv_ref[...] = jnp.zeros_like(dv_ref)

    def run(seq, tiles):
        keys = pl.ds(0, 256 * tiles)

        @pl.loop(0, NQ)
        def _(block):
            stats = g_ref[block, seq, pl.ds(192, 32), :].astype(f32)
            for h in range(3):
                q = q_ref[block, seq, pl.ds(64 * h, 64), :]
                g = g_ref[block, seq, pl.ds(64 * h, 64), :]
                rows = [one, stats[3 * h : 3 * h + 3], jnp.zeros((12, 256), f32)]
                qx = jnp.concatenate([q, jnp.concatenate(rows, 0).astype(bf16)], 0)
                rows = [stats[16 + 3 * h : 16 + 3 * h + 3], jnp.zeros((13, 256), f32)]
                gx = jnp.concatenate([g, jnp.concatenate(rows, 0).astype(bf16)], 0)
                p = jnp.exp2(jnp.dot(kx_ref[seq, h, keys, :], qx, preferred_element_type=f32))
                d = jnp.dot(vx_ref[seq, h, keys, :], gx, preferred_element_type=f32)
                ds = (p * d).astype(bf16)
                dq = jnp.dot(kt_ref[seq, h, :, keys], ds, preferred_element_type=f32)
                dk_ref[seq, h, :, keys] += lax.dot_general(q, ds, nt, preferred_element_type=f32)
                dv_ref[seq, h, :, keys] += lax.dot_general(
                    g, p.astype(bf16), nt, preferred_element_type=f32
                )
                dq_ref[block, seq, pl.ds(64 * h, 64), :] = (dq * HEAD**-0.5).astype(bf16)

    for seq in range(2):
        pick_tiles(lens_ref, place_ref, seq, run)
    for seq in range(2):
        extra = sum(g_ref[block, seq, pl.ds(192, 32), :].astype(f32) for block in range(NQ))
        extra = jnp.concatenate([extra[9:15], jnp.zeros((10, 256), f32)], 0).astype(bf16)
        for dkv_ref, (here, _) in zip((dkv0, dkv1, dkv2, dkv3), key_places(place_ref)):
            dkv_ref[seq, pl.ds(384, 16), :] = extra
            for h in range(3):
                dk = dk_ref[seq, h, :, here] * (1.0 / LOG2E)
                dkv_ref[seq, pl.ds(64 * h, 64), :] = dk.astype(bf16)
                dkv_ref[seq, pl.ds(192 + 64 * h, 64), :] = dv_ref[seq, h, :, here].astype(bf16)


def unpack_kernel(where_ref, *refs):
    first, second = refs[:5], refs[5:10]
    gate_ref, up_ref, out_ref, down_ref, norm_ref = refs[10:]
    for back_y in range(4):
        y = (where_ref[0] + 4 - back_y) % 4
        for back_z in range(4):
            z = (where_ref[1] + 4 - back_z) % 4
            index, inner = ((0, 1, 2, 4)[back_y], back_z)
            if back_y == 2 and back_z >= 2:
                index, inner = 3, back_z - 2
            for back_x in range(2):
                x = (where_ref[2] + back_x) % 2
                row = (y * 4 + z) * 2 + x
                block = first[index].at[inner, back_x]
                gate_ref[row] = block[0:3]
                up_ref[row] = block[3:6]
                block = second[index].at[inner, back_x]
                out_ref[row] = block[0:3]
                down_ref[(z * 2 + x) * 4 + y] = block[3:6]
                norm_ref[row] = block[6]


def last_kernel(
    dq_ref, d0, d1, d2, d3, cos_ref, sin_ref, tokens_ref, attn_ref, res_ref, proj_ref, grad_ref, norm_ref
):
    cosine, sine = cos_ref[...], sin_ref[...]
    grad = None
    for seq in range(2):
        dq = sum(dq_ref[block, seq].astype(f32) for block in range(NQ))
        dkv = sum(part[seq].astype(f32) for part in (d0, d1, d2, d3))
        norm_ref[seq] = dkv[384:392]
        rows = []
        for source in (dq, dkv):
            for h in range(3):
                first, second = source[64 * h : 64 * h + 32], source[64 * h + 32 : 64 * h + 64]
                rows += [first * cosine + second * sine, second * cosine - first * sine]
        rows.append(dkv[192:384])
        proj = jnp.concatenate(rows, 0).astype(bf16)
        proj_ref[seq] = proj
        wide = jnp.concatenate([proj, jnp.zeros((192, 256), bf16)], 0)
        part = lax.dot_general(
            jnp.transpose(tokens_ref[seq]), wide, (((1,), (1,)), ((), ())),
            preferred_element_type=f32,
        ) + jnp.dot(attn_ref[seq], res_ref[seq], preferred_element_type=f32)
        grad = part if grad is None else grad + part
    grad_ref[...] = grad.astype(bf16)


SMEM = pl.BlockSpec(memory_space=pltpu.SMEM)
VMEM = pl.BlockSpec(memory_space=pltpu.VMEM)
PARAMS = pltpu.CompilerParams(vmem_limit_bytes=56 * 1024 * 1024)


def attend(lengths, place, q_all, kv_all):
    return pl.pallas_call(
        attend_kernel,
        out_shape=jax.ShapeDtypeStruct((NQ, 2, 208, 256), bf16),
        in_specs=[SMEM, SMEM] + [VMEM] * 5,
        out_specs=VMEM,
        scratch_shapes=[
            pltpu.VMEM((2, 3, 1024, 80), bf16),
            pltpu.VMEM((2, 3, 80, 1024), bf16),
            pltpu.VMEM((NQ, 2, 8, 256), f32),
            pltpu.VMEM((NQ, 2, 8, 256), f32),
        ],
        compiler_params=PARAMS,
        cost_estimate=pl.CostEstimate(
            flops=23_000_000_000, bytes_accessed=5_000_000, transcendentals=12_582_912
        ),
    )(lengths, place, q_all, *kv_all)


def attend_back(lengths, place, q_all, kv_all, g_all):
    return pl.pallas_call(
        attend_back_kernel,
        out_shape=(
            jax.ShapeDtypeStruct((NQ, 2, 192, 256), bf16),
        )
        + (jax.ShapeDtypeStruct((2, 400, 256), bf16),) * NK,
        in_specs=[SMEM, SMEM] + [VMEM] * 6,
        out_specs=(VMEM,) * 5,
        scratch_shapes=[
            pltpu.VMEM((2, 3, 1024, 80), bf16),
            pltpu.VMEM((2, 3, 1024, 80), bf16),
            pltpu.VMEM((2, 3, 64, 1024), bf16),
            pltpu.VMEM((2, 3, 64, 1024), f32),
            pltpu.VMEM((2, 3, 64, 1024), f32),
        ],
        compiler_params=PARAMS,
        cost_estimate=pl.CostEstimate(
            flops=46_000_000_000, bytes_accessed=8_000_000, transcendentals=12_582_912
        ),
    )(lengths, place, q_all, *kv_all, g_all)


def unpack(where, parts):
    block = jax.ShapeDtypeStruct((32, 3, 8, 768), bf16)
    *weights, norms = pl.pallas_call(
        unpack_kernel,
        out_shape=(block,) * 4 + (jax.ShapeDtypeStruct((32, 8, 768), bf16),),
        in_specs=[SMEM] + [VMEM] * 10,
        out_specs=(VMEM,) * 5,
        compiler_params=PARAMS,
        cost_estimate=pl.CostEstimate(flops=0, bytes_accessed=12_000_000, transcendentals=0),
    )(where, *parts)
    return [weight.reshape(768, 768) for weight in weights], norms


def last(dq, dkv, cosine, sine, tokens, attn, res):
    return pl.pallas_call(
        last_kernel,
        out_shape=(
            jax.ShapeDtypeStruct((2, 576, 256), bf16),
            jax.ShapeDtypeStruct((768, 768), bf16),
            jax.ShapeDtypeStruct((2, 8, 256), f32),
        ),
        in_specs=[VMEM] * 10,
        out_specs=(VMEM,) * 3,
        compiler_params=PARAMS,
        cost_estimate=pl.CostEstimate(
            flops=1_300_000_000, bytes_accessed=8_000_000, transcendentals=0
        ),
    )(dq, *dkv, cosine, sine, tokens, attn, res)


def on_device(hidden_in, lengths, w_qkv, w_out, w_gate, w_up, w_down, norm_params, cotangent):
    y_i, z_i, xh_i = (lax.axis_index(a) for a in WIDE)
    wide_i = (y_i * 4 + z_i) * 2 + xh_i
    n_i = lax.axis_index("xl") * 2 + lax.axis_index("c")
    seqs, own_slots, width = hidden_in.shape
    slots = own_slots * 4

    pair = in_order(hidden_in, flip(hidden_in, "xl"), lax.axis_index("xl"))
    tokens = in_order(pair, flip(pair, "c"), lax.axis_index("c"))
    tokens = tokens.transpose(2, 1, 0, 3, 4).reshape(seqs, slots, width)

    first_z = round_x_z(jnp.concatenate([w_gate, w_up]))
    sent = []
    for to in range(4):
        pick = (to - 3 * n_i) % 4
        block = jnp.where(
            pick == 0, w_qkv[:, :192], jnp.where(pick == 1, w_qkv[:, 192:384], w_qkv[:, 384:])
        )
        norm_row = jnp.pad(norm_params, ((0, 7), (0, 168)))
        sent.append(jnp.concatenate([block, w_out, w_down[24 * to : 24 * to + 24], norm_row]))
    got = exchange(jnp.stack(sent), NARROW)
    sources = (4 * jnp.arange(3) + n_i) // 3
    qkv_mine = jnp.take(got[:, :24], sources, axis=0).transpose(1, 0, 2).reshape(24, 576)
    wqkv = gather(qkv_mine, WIDE, 32).reshape(width, 576)

    turn_pairs = [((y * 4 + n), (n * 4 + y)) for y in range(4) for n in range(4)]
    down_rows = got[:, 48:72].transpose(1, 0, 2).reshape(24, width)
    down_rows = lax.ppermute(down_rows, ("y",) + NARROW, turn_pairs)
    out_rows = got[:, 24:48].transpose(1, 0, 2).reshape(24, width)
    norm_row = jnp.pad(got[:, 72, :24].reshape(1, 96), ((0, 7), (0, width - 96)))
    second_z = round_x_z(jnp.concatenate([out_rows, down_rows, norm_row]))
    first_rows = jnp.stack(first_z)
    first_parts = round_y(first_rows)
    wqkv = after(wqkv, first_rows, second_z[0])

    positions = wide_i * slots + jnp.arange(slots)
    freqs = 10000.0 ** (-2.0 * jnp.arange(HEAD // 2, dtype=f32) / HEAD)
    angles = freqs[:, None] * positions.astype(f32)[None, :]
    cosine, sine = jnp.cos(angles), jnp.sin(angles)
    projected = jnp.einsum("df,std->sft", wqkv, tokens, preferred_element_type=f32)

    def rotate(block):
        halves = block.reshape(seqs, 3, 2, HEAD // 2, slots)
        first, second = halves[:, :, 0], halves[:, :, 1]
        return jnp.stack(
            [first * cosine - second * sine, second * cosine + first * sine], 2
        ).reshape(seqs, 192, slots)

    query = (rotate(projected[:, :192]) * (HEAD**-0.5 * LOG2E)).astype(bf16)
    keyval = jnp.concatenate(
        [rotate(projected[:, 192:384]), projected[:, 384:]], axis=1
    ).astype(bf16)
    q_all = gather(query, QAX, NQ)
    kv_all = [keyval] + [along(keyval, "y", back) for back in range(1, NK)]
    second_parts = round_y(jnp.stack(after(second_z, kv_all[1])))
    place = jnp.stack([y_i, (z_i * 2 + xh_i) * slots]).astype(jnp.int32)
    place = after(place, first_parts[1], first_parts[4])
    parts = attend(lengths, place, q_all, kv_all)
    parts = after(parts, *first_parts, second_parts[1], second_parts[4])
    parts = exchange(parts, QAX).astype(f32)
    part_lse = jnp.sum(parts[:, :, 192:201].reshape(NQ, seqs, 3, 3, slots), 2)
    top = jnp.max(part_lse, 0)
    lse = top + jnp.log2(jnp.sum(jnp.exp2(part_lse - top), 0))
    shares = jnp.exp2(part_lse - lse)
    where = jnp.stack([y_i, z_i, xh_i]).astype(jnp.int32)
    (wgate, wup, wout, wdown), norms = unpack(where, first_parts + second_parts)
    norm_values = (
        norms[:, 0, :96].reshape(32, 4, 24).transpose(1, 0, 2).reshape(4, width).astype(f32)
    )
    attended = jnp.sum(
        parts[:, :, :192].reshape(NQ, seqs, 3, HEAD, slots) * shares[:, :, :, None, :], 0
    )
    attn_sent = attended.reshape(seqs, 192, slots).astype(bf16)
    attn_all = narrow_gather(attn_sent)

    projection = jnp.einsum("sft,fd->std", attn_all, wout, preferred_element_type=f32)
    normed, _, _ = layer_norm_parts(
        tokens.astype(f32) + projection, norm_values[0], norm_values[1]
    )
    normed_low = normed.astype(bf16)
    own_slice = lambda a: lax.dynamic_slice_in_dim(a, n_i * own_slots, own_slots, 1)
    own_first, unit_first, inv_first = layer_norm_parts(
        hidden_in.astype(f32) + own_slice(projection), norm_values[0], norm_values[1]
    )
    flat_low = normed_low.reshape(-1, width)
    gate_pre = jnp.dot(flat_low, wgate, preferred_element_type=f32)
    up_pre = jnp.dot(flat_low, wup, preferred_element_type=f32)
    gate_sigmoid = jax.nn.sigmoid(gate_pre)
    gate_silu = gate_pre * gate_sigmoid
    activated = (gate_silu * up_pre).astype(bf16)
    down_part = jnp.dot(activated, wdown, preferred_element_type=f32)
    down_out = sum_to_own(down_part.reshape(seqs, slots, width))
    output_rows, unit_second, inv_second = layer_norm_parts(
        own_first + down_out, norm_values[2], norm_values[3]
    )
    own_positions = wide_i * slots + n_i * own_slots + jnp.arange(own_slots)
    valid = (own_positions[None, :] < lengths[:, None]).astype(f32)[:, :, None]
    layer_out = (output_rows * valid).astype(bf16)
    grad_rows = cotangent.astype(f32) * valid
    grad_gain2 = jnp.sum(grad_rows * unit_second, (0, 1))
    grad_bias2 = jnp.sum(grad_rows, (0, 1))
    grad_second = norm_back(grad_rows, unit_second, inv_second, norm_values[2])
    down_low = narrow_gather(grad_second.astype(bf16)).reshape(-1, width)

    grad_wdown = jnp.einsum("tf,td->fd", activated, down_low, preferred_element_type=f32)
    grad_act = jnp.einsum("td,fd->tf", down_low, wdown, preferred_element_type=f32)
    silu_slope = gate_sigmoid * (1.0 + gate_pre * (1.0 - gate_sigmoid))
    grad_gate_low = (grad_act * up_pre * silu_slope).astype(bf16)
    grad_up_low = (grad_act * gate_silu).astype(bf16)
    grad_wgate = jnp.einsum("td,tf->df", flat_low, grad_gate_low, preferred_element_type=f32)
    grad_wup = jnp.einsum("td,tf->df", flat_low, grad_up_low, preferred_element_type=f32)
    first_part = jnp.einsum(
        "tf,df->td", grad_gate_low, wgate, preferred_element_type=f32
    ) + jnp.einsum("tf,df->td", grad_up_low, wup, preferred_element_type=f32)
    grad_normed = grad_second + sum_to_own(first_part.reshape(seqs, slots, width))
    grad_gain1 = jnp.sum(grad_normed * unit_first, (0, 1))
    grad_bias1 = jnp.sum(grad_normed, (0, 1))
    grad_first = norm_back(grad_normed, unit_first, inv_first, norm_values[0])
    res_low = narrow_gather(grad_first.astype(bf16))
    out_mine = lax.dynamic_slice_in_dim(wout, n_i * 192, 192, 0)
    grad_attn = jnp.einsum("fd,std->sft", out_mine, res_low, preferred_element_type=f32).astype(
        bf16
    )
    delta = jnp.sum(
        grad_attn.astype(f32).reshape(seqs, 3, HEAD, slots) * attended, 2
    )

    def three(x):
        hi = lax.reduce_precision(x, 8, 7)
        mid = lax.reduce_precision(x - hi, 8, 7)
        low = x - hi - mid
        return jnp.stack([hi, mid, low], 2).reshape(seqs, 9, slots).astype(bf16)

    grad_norm_rows = jnp.stack([grad_gain1, grad_bias1, grad_gain2, grad_bias2])
    sent_back = jnp.concatenate(
        [
            grad_attn,
            three(-lse),
            grad_norm_rows.reshape(seqs, 6, slots).astype(bf16),
            jnp.zeros((seqs, 1, slots), bf16),
            three(-delta),
            jnp.zeros((seqs, 7, slots), bf16),
        ],
        axis=1,
    )
    g_all = gather(sent_back, QAX, NQ)

    grads_packed = jnp.concatenate(
        [
            grad_wgate.astype(bf16).reshape(32, 24, width),
            grad_wup.astype(bf16).reshape(32, 24, width),
            grad_wdown.astype(bf16)
            .reshape(8, 4, 24, width)
            .transpose(1, 0, 2, 3)
            .reshape(32, 24, width),
        ],
        axis=1,
    )
    grads_packed, g_all = lax.optimization_barrier((grads_packed, g_all))
    grads_got = exchange(grads_packed, WIDE)
    dq_parts, *dkv_parts = attend_back(lengths, place, q_all, kv_all, g_all)
    grads_got, dq_parts, dkv_parts = lax.optimization_barrier((grads_got, dq_parts, dkv_parts))
    grads_got = jnp.sum(grads_got.astype(f32), 0)
    sum_gate = grads_got[0:24]
    sum_up = grads_got[24:48]
    down_rows = lax.ppermute(grads_got[48:72].astype(bf16), ("y",) + NARROW, turn_pairs)

    dkv_got = [dkv_parts[0]] + [along(dkv_parts[back], "y", NK - back) for back in range(1, NK)]
    res_cols = jnp.pad(
        lax.dynamic_slice_in_dim(res_low, n_i * 192, 192, 2), ((0, 0), (0, 0), (576, 0))
    )
    grad_proj, grad_last, norm_sums = last(
        exchange(dq_parts, QAX), dkv_got, cosine, sine, tokens, attn_all, res_cols
    )
    norm_sums = norm_sums[:, :6].reshape(4, 32, 24)
    norm_sums = lax.dynamic_index_in_dim(norm_sums, wide_i, 1, keepdims=False)
    input_part = jnp.einsum("sft,df->std", grad_proj, wqkv, preferred_element_type=f32)
    grad_input = (grad_first + sum_to_own(input_part)).astype(bf16)
    last_got = jnp.sum(exchange(grad_last.reshape(32, 24, width), WIDE).astype(f32), 0)
    sum_out = last_got[:, 576:]
    back = last_got[:, :576].reshape(24, 3, 192).transpose(1, 0, 2)
    to = (sources[None, :] == jnp.arange(4)[:, None]).astype(f32)
    back_sent = jnp.einsum("sk,kdf->sdf", to, back).astype(bf16)
    norm_sent = jnp.pad(norm_sums[:, None, :], ((0, 0), (0, 7), (0, 168))).astype(bf16)
    down_sent = down_rows.reshape(24, 4, 192).transpose(1, 0, 2)
    back_got = exchange(jnp.concatenate([back_sent, down_sent, norm_sent], 1), NARROW).astype(f32)
    sum_down = back_got[:, 24:48].reshape(96, 192)
    sum_norms = jnp.sum(back_got[:, 48, :24], 0)[None]
    order = (3 * n_i + jnp.arange(3)) % 4
    sum_qkv = jnp.take(back_got[:, :24], order, axis=0).transpose(1, 0, 2).reshape(24, 576)
    return (layer_out, grad_input, sum_qkv, sum_out, sum_gate, sum_up, sum_down, sum_norms)


def solution(mesh):
    fine = Mesh(mesh.devices.reshape(4, 4, 2, 2, 2), AXES)
    token = P(None, WIDE + NARROW, None)
    weight = P(WIDE, NARROW)
    norm = P(NARROW, WIDE)
    return jax.shard_map(
        on_device,
        mesh=fine,
        in_specs=(token, P(), weight, weight, weight, weight, weight, norm, token),
        out_specs=(token, token, weight, weight, weight, weight, weight, norm),
        check_vma=False,
    )
```

```python
import functools
import math

import jax
import jax.numpy as jnp
from jax import lax
from jax.experimental import pallas as pl
from jax.experimental.pallas import tpu as pltpu
from jax.sharding import Mesh
from jax.sharding import PartitionSpec as P

HEADS = 12
HEAD = 64
EPSILON = 1e-05
AXES = ("y", "z", "xh", "xl", "c")
WIDE = ("y", "z", "xh")
NARROW = ("xl", "c")
QAX = ("z", "xh")
NQ = 8
NK = 4
STEP = 4
LOG2E = math.log2(math.e)
NEG = -1e30
f32 = jnp.float32
bf16 = jnp.bfloat16


def exchange(x, axes):
    return lax.all_to_all(x, axes, 0, 0, tiled=True)


def gather(x, axes, n):
    return exchange(jnp.broadcast_to(x[None], (n,) + x.shape), axes)


def along(x, axis, by):
    return lax.ppermute(x, axis, [(i, (i + by) % 4) for i in range(4)])


def after(x, *others):
    return lax.optimization_barrier((x,) + others)[0]


def round_x_z(rows):
    rows = rows.reshape(-1, 8, rows.shape[-1])
    arrived = flip(rows, "xh")
    rows = jnp.stack([rows, arrived])
    return [rows] + [along(rows, "z", back) for back in range(1, 4)], arrived


def round_y(rows):
    before, behind = along(rows, "y", 1), along(rows, "y", 3)
    return [rows, before, along(before[:2], "y", 1), along(behind[2:], "y", 3), behind]


def entry(x, index):
    return lax.dynamic_index_in_dim(x, index, 0, keepdims=False)


def in_order(mine, other, index):
    return jnp.stack([jnp.where(index == 0, mine, other), jnp.where(index == 0, other, mine)])


def flip(x, axis):
    return lax.ppermute(x, axis, [(0, 1), (1, 0)])


def layer_norm_parts(residual, gain_vec, bias_vec):
    row_mean = jnp.mean(residual, -1, keepdims=True)
    centred = residual - row_mean
    variance = jnp.mean(centred * centred, -1, keepdims=True)
    inv_std = lax.rsqrt(variance + EPSILON)
    unit_rows = centred * inv_std
    return (unit_rows * gain_vec + bias_vec, unit_rows, inv_std)


def norm_back(incoming, unit_rows, inv_std, gain_vec):
    scaled = incoming * gain_vec
    return inv_std * (
        scaled
        - jnp.mean(scaled, -1, keepdims=True)
        - unit_rows * jnp.mean(scaled * unit_rows, -1, keepdims=True)
    )


def sum_to_own(part):
    seqs, slots, width = part.shape
    cells = part.reshape(seqs, 2, 2, slots // 4, width)
    ci, xi = lax.axis_index("c"), lax.axis_index("xl")
    mine = lax.dynamic_index_in_dim(cells, ci, 2, keepdims=False)
    theirs = lax.dynamic_index_in_dim(cells, 1 - ci, 2, keepdims=False)
    half = mine.astype(f32) + flip(theirs.astype(bf16), "c").astype(f32)
    mine = lax.dynamic_index_in_dim(half, xi, 1, keepdims=False)
    theirs = lax.dynamic_index_in_dim(half, 1 - xi, 1, keepdims=False)
    return mine + flip(theirs.astype(bf16), "xl").astype(f32)


def narrow_gather(x):
    return lax.all_gather(x, NARROW, axis=1, tiled=True)


def split3(x):
    hi = x.astype(bf16)
    rest = x - hi.astype(f32)
    mid = rest.astype(bf16)
    low = (rest - mid.astype(f32)).astype(bf16)
    return hi, mid, low


def key_bias(lens_ref, start, seq):
    slot = start + lax.broadcasted_iota(jnp.int32, (16, 256), 1)
    row = lax.broadcasted_iota(jnp.int32, (16, 256), 0)
    bias = jnp.where(slot < lens_ref[seq], 0.0, NEG)
    return jnp.where(row == 0, bias, jnp.where(row < 4, 1.0, 0.0)).astype(bf16)


def key_places(place_ref):
    places = []
    for back in range(NK):
        row = (place_ref[0] + NK - back) % NK
        places.append((pl.ds(pl.multiple_of(256 * row, 256), 256), place_ref[1] + 2048 * row))
    return places


def pick_tiles(lens_ref, place_ref, seq, run):
    n = jnp.int32(0)
    for tile in range(NK):
        n = n + (place_ref[1] + 2048 * tile < lens_ref[seq]).astype(jnp.int32)
    for tiles in range(1, NK + 1):
        pl.when(n == tiles)(functools.partial(run, seq, tiles))


def attend_kernel(
    lens_ref, place_ref, q_ref, kv0, kv1, kv2, kv3, out_ref, kx_ref, vx_ref, sum_ref, peak_ref
):
    row = lax.broadcasted_iota(jnp.int32, (16, 256), 0)
    one_row = jnp.where(row == 0, 1.0, 0.0).astype(bf16)
    one_rows = jnp.concatenate([one_row] * STEP, 1)
    for seq in range(2):
        for kv_ref, (here, start) in zip((kv0, kv1, kv2, kv3), key_places(place_ref)):
            extra = key_bias(lens_ref, start, seq)
            for h in range(3):
                kt = jnp.concatenate([kv_ref[seq, pl.ds(64 * h, 64), :], extra], 0)
                kx_ref[seq, h, here, :] = jnp.transpose(kt)
                vx_ref[seq, h, pl.ds(0, 64), here] = kv_ref[seq, pl.ds(192 + 64 * h, 64), :]
                vx_ref[seq, h, pl.ds(64, 16), here] = one_row

    def run(seq, tiles, bounded):
        keys = pl.ds(0, 256 * tiles)

        @pl.loop(0, NQ // STEP)
        def _(turn):
            for h in range(3):
                q = [q_ref[turn * STEP + j, seq, pl.ds(64 * h, 64), :] for j in range(STEP)]
                qx = jnp.concatenate([jnp.concatenate(q, 1), one_rows], 0)
                s = jnp.dot(kx_ref[seq, h, keys, :], qx, preferred_element_type=f32)
                if bounded:
                    peak = jnp.zeros((1, 256 * STEP), f32)
                    p = jnp.exp2(s).astype(bf16)
                else:
                    peak = jnp.max(s, 0, keepdims=True)
                    p = jnp.exp2(s - peak).astype(bf16)
                o = jnp.dot(vx_ref[seq, h, :, keys], p, preferred_element_type=f32)
                total = o[64:65]
                o = (o[:64] * (1.0 / total)).astype(bf16)
                for j in range(STEP):
                    here = slice(256 * j, 256 * j + 256)
                    out_ref[turn * STEP + j, seq, pl.ds(64 * h, 64), :] = o[:, here]
                    sum_ref[turn * STEP + j, seq, pl.ds(h, 1), :] = total[:, here]
                    peak_ref[turn * STEP + j, seq, pl.ds(h, 1), :] = peak[:, here]

    top_key = jnp.zeros((1, 256), f32)
    for kv_ref in (kv0, kv1, kv2, kv3):
        for seq in range(2):
            for h in range(3):
                k = kv_ref[seq, pl.ds(64 * h, 64), :].astype(f32)
                top_key = jnp.maximum(top_key, jnp.sum(k * k, 0, keepdims=True))

    def widest(block, top):
        for seq in range(2):
            for h in range(3):
                q = q_ref[block, seq, pl.ds(64 * h, 64), :].astype(f32)
                top = jnp.maximum(top, jnp.sum(q * q, 0, keepdims=True))
        return top

    top_query = lax.fori_loop(0, NQ, widest, jnp.zeros((1, 256), f32))
    bounded = jnp.max(top_key) * jnp.max(top_query) < 100.0**2

    @pl.when(bounded)
    def _():
        for seq in range(2):
            pick_tiles(lens_ref, place_ref, seq, functools.partial(run, bounded=True))

    @pl.when(jnp.logical_not(bounded))
    def _():
        for seq in range(2):
            run(seq, NK, False)

    for seq in range(2):
        for block in range(NQ):
            lse = peak_ref[block, seq, pl.ds(0, 3), :] + jnp.log2(sum_ref[block, seq, pl.ds(0, 3), :])
            rows = [part.astype(f32) for part in split3(lse)] + [jnp.zeros((7, 256), f32)]
            out_ref[block, seq, pl.ds(192, 16), :] = jnp.concatenate(rows, 0).astype(bf16)


def attend_back_kernel(
    lens_ref, place_ref, q_ref, kv0, kv1, kv2, kv3, g_ref, dq_ref, dkv0, dkv1, dkv2, dkv3,
    kx_ref, vx_ref, kt_ref, dk_ref, dv_ref,
):
    row = lax.broadcasted_iota(jnp.int32, (16, 256), 0)
    ones = jnp.where(row < 3, 1.0, 0.0).astype(bf16)
    one = jnp.ones((1, 256), f32)
    nt = (((1,), (1,)), ((), ()))
    for seq in range(2):
        for kv_ref, (here, start) in zip((kv0, kv1, kv2, kv3), key_places(place_ref)):
            extra = key_bias(lens_ref, start, seq)
            for h in range(3):
                k = kv_ref[seq, pl.ds(64 * h, 64), :]
                v = kv_ref[seq, pl.ds(192 + 64 * h, 64), :]
                kx_ref[seq, h, here, :] = jnp.transpose(jnp.concatenate([k, extra], 0))
                vx_ref[seq, h, here, :] = jnp.transpose(jnp.concatenate([v, ones], 0))
                kt_ref[seq, h, :, here] = k
    dk_ref[...] = jnp.zeros_like(dk_ref)
    dv_ref[...] = jnp.zeros_like(dv_ref)

    def run(seq, tiles):
        keys = pl.ds(0, 256 * tiles)

        @pl.loop(0, NQ)
        def _(block):
            stats = g_ref[block, seq, pl.ds(192, 32), :].astype(f32)
            for h in range(3):
                q = q_ref[block, seq, pl.ds(64 * h, 64), :]
                g = g_ref[block, seq, pl.ds(64 * h, 64), :]
                rows = [one, stats[3 * h : 3 * h + 3], jnp.zeros((12, 256), f32)]
                qx = jnp.concatenate([q, jnp.concatenate(rows, 0).astype(bf16)], 0)
                rows = [stats[16 + 3 * h : 16 + 3 * h + 3], jnp.zeros((13, 256), f32)]
                gx = jnp.concatenate([g, jnp.concatenate(rows, 0).astype(bf16)], 0)
                p = jnp.exp2(jnp.dot(kx_ref[seq, h, keys, :], qx, preferred_element_type=f32))
                d = jnp.dot(vx_ref[seq, h, keys, :], gx, preferred_element_type=f32)
                ds = (p * d).astype(bf16)
                dq = jnp.dot(kt_ref[seq, h, :, keys], ds, preferred_element_type=f32)
                dk_ref[seq, h, :, keys] += lax.dot_general(q, ds, nt, preferred_element_type=f32)
                dv_ref[seq, h, :, keys] += lax.dot_general(
                    g, p.astype(bf16), nt, preferred_element_type=f32
                )
                dq_ref[block, seq, pl.ds(64 * h, 64), :] = (dq * HEAD**-0.5).astype(bf16)

    for seq in range(2):
        pick_tiles(lens_ref, place_ref, seq, run)
    for seq in range(2):
        extra = sum(g_ref[block, seq, pl.ds(192, 32), :].astype(f32) for block in range(NQ))
        extra = jnp.concatenate([extra[9:15], jnp.zeros((10, 256), f32)], 0).astype(bf16)
        for dkv_ref, (here, _) in zip((dkv0, dkv1, dkv2, dkv3), key_places(place_ref)):
            dkv_ref[seq, pl.ds(384, 16), :] = extra
            for h in range(3):
                dk = dk_ref[seq, h, :, here] * (1.0 / LOG2E)
                dkv_ref[seq, pl.ds(64 * h, 64), :] = dk.astype(bf16)
                dkv_ref[seq, pl.ds(192 + 64 * h, 64), :] = dv_ref[seq, h, :, here].astype(bf16)


def unpack_kernel(where_ref, *refs):
    first, second = refs[:5], refs[5:10]
    gate_ref, up_ref, out_ref, down_ref, norm_ref = refs[10:]
    for back_y in range(4):
        y = (where_ref[0] + 4 - back_y) % 4
        for back_z in range(4):
            z = (where_ref[1] + 4 - back_z) % 4
            index, inner = ((0, 1, 2, 4)[back_y], back_z)
            if back_y == 2 and back_z >= 2:
                index, inner = 3, back_z - 2
            for back_x in range(2):
                x = (where_ref[2] + back_x) % 2
                row = (y * 4 + z) * 2 + x
                block = first[index].at[inner, back_x]
                gate_ref[row] = block[0:3]
                up_ref[row] = block[3:6]
                block = second[index].at[inner, back_x]
                out_ref[row] = block[0:3]
                down_ref[(z * 2 + x) * 4 + y] = block[3:6]
                norm_ref[row] = block[6]


def last_kernel(
    dq_ref, d0, d1, d2, d3, cos_ref, sin_ref, tokens_ref, attn_ref, res_ref, proj_ref, grad_ref, norm_ref
):
    cosine, sine = cos_ref[...], sin_ref[...]
    grad = None
    for seq in range(2):
        dq = sum(dq_ref[block, seq].astype(f32) for block in range(NQ))
        dkv = sum(part[seq].astype(f32) for part in (d0, d1, d2, d3))
        norm_ref[seq] = dkv[384:392]
        rows = []
        for source in (dq, dkv):
            for h in range(3):
                first, second = source[64 * h : 64 * h + 32], source[64 * h + 32 : 64 * h + 64]
                rows += [first * cosine + second * sine, second * cosine - first * sine]
        rows.append(dkv[192:384])
        proj = jnp.concatenate(rows, 0).astype(bf16)
        proj_ref[seq] = proj
        wide = jnp.concatenate([proj, jnp.zeros((192, 256), bf16)], 0)
        part = lax.dot_general(
            jnp.transpose(tokens_ref[seq]), wide, (((1,), (1,)), ((), ())),
            preferred_element_type=f32,
        ) + jnp.dot(attn_ref[seq], res_ref[seq], preferred_element_type=f32)
        grad = part if grad is None else grad + part
    grad_ref[...] = grad.astype(bf16)


SMEM = pl.BlockSpec(memory_space=pltpu.SMEM)
VMEM = pl.BlockSpec(memory_space=pltpu.VMEM)
PARAMS = pltpu.CompilerParams(vmem_limit_bytes=56 * 1024 * 1024)


def attend(lengths, place, q_all, kv_all):
    return pl.pallas_call(
        attend_kernel,
        out_shape=jax.ShapeDtypeStruct((NQ, 2, 208, 256), bf16),
        in_specs=[SMEM, SMEM] + [VMEM] * 5,
        out_specs=VMEM,
        scratch_shapes=[
            pltpu.VMEM((2, 3, 1024, 80), bf16),
            pltpu.VMEM((2, 3, 80, 1024), bf16),
            pltpu.VMEM((NQ, 2, 8, 256), f32),
            pltpu.VMEM((NQ, 2, 8, 256), f32),
        ],
        compiler_params=PARAMS,
        cost_estimate=pl.CostEstimate(
            flops=23_000_000_000, bytes_accessed=5_000_000, transcendentals=12_582_912
        ),
    )(lengths, place, q_all, *kv_all)


def attend_back(lengths, place, q_all, kv_all, g_all):
    return pl.pallas_call(
        attend_back_kernel,
        out_shape=(
            jax.ShapeDtypeStruct((NQ, 2, 192, 256), bf16),
        )
        + (jax.ShapeDtypeStruct((2, 400, 256), bf16),) * NK,
        in_specs=[SMEM, SMEM] + [VMEM] * 6,
        out_specs=(VMEM,) * 5,
        scratch_shapes=[
            pltpu.VMEM((2, 3, 1024, 80), bf16),
            pltpu.VMEM((2, 3, 1024, 80), bf16),
            pltpu.VMEM((2, 3, 64, 1024), bf16),
            pltpu.VMEM((2, 3, 64, 1024), f32),
            pltpu.VMEM((2, 3, 64, 1024), f32),
        ],
        compiler_params=PARAMS,
        cost_estimate=pl.CostEstimate(
            flops=46_000_000_000, bytes_accessed=8_000_000, transcendentals=12_582_912
        ),
    )(lengths, place, q_all, *kv_all, g_all)


def unpack(where, parts):
    block = jax.ShapeDtypeStruct((32, 3, 8, 768), bf16)
    *weights, norms = pl.pallas_call(
        unpack_kernel,
        out_shape=(block,) * 4 + (jax.ShapeDtypeStruct((32, 8, 768), bf16),),
        in_specs=[SMEM] + [VMEM] * 10,
        out_specs=(VMEM,) * 5,
        compiler_params=PARAMS,
        cost_estimate=pl.CostEstimate(flops=0, bytes_accessed=12_000_000, transcendentals=0),
    )(where, *parts)
    return [weight.reshape(768, 768) for weight in weights], norms


def last(dq, dkv, cosine, sine, tokens, attn, res):
    return pl.pallas_call(
        last_kernel,
        out_shape=(
            jax.ShapeDtypeStruct((2, 576, 256), bf16),
            jax.ShapeDtypeStruct((768, 768), bf16),
            jax.ShapeDtypeStruct((2, 8, 256), f32),
        ),
        in_specs=[VMEM] * 10,
        out_specs=(VMEM,) * 3,
        compiler_params=PARAMS,
        cost_estimate=pl.CostEstimate(
            flops=1_300_000_000, bytes_accessed=8_000_000, transcendentals=0
        ),
    )(dq, *dkv, cosine, sine, tokens, attn, res)


def on_device(hidden_in, lengths, w_qkv, w_out, w_gate, w_up, w_down, norm_params, cotangent):
    y_i, z_i, xh_i = (lax.axis_index(a) for a in WIDE)
    wide_i = (y_i * 4 + z_i) * 2 + xh_i
    n_i = lax.axis_index("xl") * 2 + lax.axis_index("c")
    seqs, own_slots, width = hidden_in.shape
    slots = own_slots * 4

    first_z, _ = round_x_z(jnp.concatenate([w_gate, w_up]))
    sent = []
    for to in range(4):
        pick = (to - 3 * n_i) % 4
        block = jnp.where(
            pick == 0, w_qkv[:, :192], jnp.where(pick == 1, w_qkv[:, 192:384], w_qkv[:, 384:])
        )
        norm_row = jnp.pad(norm_params, ((0, 7), (0, 168)))
        sent.append(jnp.concatenate([block, w_out, w_down[24 * to : 24 * to + 24], norm_row]))
    sent = jnp.stack(sent)
    got = exchange(sent, NARROW)
    sources = [(4 * k + n_i) // 3 for k in range(3)]
    qkv_mine = jnp.concatenate([entry(got[:, :24], source) for source in sources], axis=1)
    wqkv = gather(qkv_mine, WIDE, 32).reshape(width, 576)

    pair = in_order(hidden_in, flip(after(hidden_in, sent), "xl"), lax.axis_index("xl"))
    tokens = in_order(pair, flip(pair, "c"), lax.axis_index("c"))
    tokens = tokens.transpose(2, 1, 0, 3, 4).reshape(seqs, slots, width)

    turn_pairs = [((y * 4 + n), (n * 4 + y)) for y in range(4) for n in range(4)]
    down_rows = got[:, 48:72].transpose(1, 0, 2).reshape(24, width)
    down_rows = lax.ppermute(down_rows, ("y",) + NARROW, turn_pairs)
    out_rows = got[:, 24:48].transpose(1, 0, 2).reshape(24, width)
    norm_row = jnp.pad(got[:, 72, :24].reshape(1, 96), ((0, 7), (0, width - 96)))
    second_z, second_x = round_x_z(jnp.concatenate([out_rows, down_rows, norm_row]))
    first_rows = jnp.stack(first_z)
    first_parts = round_y(first_rows)
    wqkv = after(wqkv, *first_z[1:], second_x)

    positions = wide_i * slots + jnp.arange(slots)
    freqs = 10000.0 ** (-2.0 * jnp.arange(HEAD // 2, dtype=f32) / HEAD)
    angles = freqs[:, None] * positions.astype(f32)[None, :]
    cosine, sine = jnp.cos(angles), jnp.sin(angles)
    projected = jnp.einsum("df,std->sft", wqkv, tokens, preferred_element_type=f32)

    def rotate(block):
        halves = block.reshape(seqs, 3, 2, HEAD // 2, slots)
        first, second = halves[:, :, 0], halves[:, :, 1]
        return jnp.stack(
            [first * cosine - second * sine, second * cosine + first * sine], 2
        ).reshape(seqs, 192, slots)

    query = (rotate(projected[:, :192]) * (HEAD**-0.5 * LOG2E)).astype(bf16)
    keyval = jnp.concatenate(
        [rotate(projected[:, 192:384]), projected[:, 384:]], axis=1
    ).astype(bf16)
    q_all = gather(query, QAX, NQ)
    kv_all = [keyval] + [along(keyval, "y", back) for back in range(1, NK)]
    second_parts = round_y(jnp.stack(after(second_z, kv_all[1])))
    place = jnp.stack([y_i, (z_i * 2 + xh_i) * slots]).astype(jnp.int32)
    place = after(place, first_parts[1], first_parts[4])
    parts = attend(lengths, place, q_all, kv_all)
    parts = after(parts, *first_parts, second_parts[1], second_parts[4])
    parts = exchange(parts, QAX).astype(f32)
    part_lse = jnp.sum(parts[:, :, 192:201].reshape(NQ, seqs, 3, 3, slots), 2)
    top = jnp.max(part_lse, 0)
    lse = top + jnp.log2(jnp.sum(jnp.exp2(part_lse - top), 0))
    shares = jnp.exp2(part_lse - lse)
    where = jnp.stack([y_i, z_i, xh_i]).astype(jnp.int32)
    (wgate, wup, wout, wdown), norms = unpack(where, first_parts + second_parts)
    norm_values = (
        norms[:, 0, :96].reshape(32, 4, 24).transpose(1, 0, 2).reshape(4, width).astype(f32)
    )
    attended = jnp.sum(
        parts[:, :, :192].reshape(NQ, seqs, 3, HEAD, slots) * shares[:, :, :, None, :], 0
    )
    attn_sent = attended.reshape(seqs, 192, slots).astype(bf16)
    attn_all = narrow_gather(attn_sent)

    projection = jnp.einsum("sft,fd->std", attn_all, wout, preferred_element_type=f32)
    normed, _, _ = layer_norm_parts(
        tokens.astype(f32) + projection, norm_values[0], norm_values[1]
    )
    normed_low = normed.astype(bf16)
    own_slice = lambda a: lax.dynamic_slice_in_dim(a, n_i * own_slots, own_slots, 1)
    own_first, unit_first, inv_first = layer_norm_parts(
        hidden_in.astype(f32) + own_slice(projection), norm_values[0], norm_values[1]
    )
    flat_low = normed_low.reshape(-1, width)
    gate_pre = jnp.dot(flat_low, wgate, preferred_element_type=f32)
    up_pre = jnp.dot(flat_low, wup, preferred_element_type=f32)
    gate_sigmoid = jax.nn.sigmoid(gate_pre)
    gate_silu = gate_pre * gate_sigmoid
    activated = (gate_silu * up_pre).astype(bf16)
    down_part = jnp.dot(activated, wdown, preferred_element_type=f32)
    down_out = sum_to_own(down_part.reshape(seqs, slots, width))
    output_rows, unit_second, inv_second = layer_norm_parts(
        own_first + down_out, norm_values[2], norm_values[3]
    )
    own_positions = wide_i * slots + n_i * own_slots + jnp.arange(own_slots)
    valid = (own_positions[None, :] < lengths[:, None]).astype(f32)[:, :, None]
    layer_out = (output_rows * valid).astype(bf16)
    grad_rows = cotangent.astype(f32) * valid
    grad_gain2 = jnp.sum(grad_rows * unit_second, (0, 1))
    grad_bias2 = jnp.sum(grad_rows, (0, 1))
    grad_second = norm_back(grad_rows, unit_second, inv_second, norm_values[2])
    down_low = narrow_gather(grad_second.astype(bf16)).reshape(-1, width)

    grad_wdown = jnp.einsum("tf,td->fd", activated, down_low, preferred_element_type=f32)
    grad_act = jnp.einsum("td,fd->tf", down_low, wdown, preferred_element_type=f32)
    silu_slope = gate_sigmoid * (1.0 + gate_pre * (1.0 - gate_sigmoid))
    grad_gate_low = (grad_act * up_pre * silu_slope).astype(bf16)
    grad_up_low = (grad_act * gate_silu).astype(bf16)
    grad_wgate = jnp.einsum("td,tf->df", flat_low, grad_gate_low, preferred_element_type=f32)
    grad_wup = jnp.einsum("td,tf->df", flat_low, grad_up_low, preferred_element_type=f32)
    first_part = jnp.einsum(
        "tf,df->td", grad_gate_low, wgate, preferred_element_type=f32
    ) + jnp.einsum("tf,df->td", grad_up_low, wup, preferred_element_type=f32)
    grad_normed = grad_second + sum_to_own(first_part.reshape(seqs, slots, width))
    grad_gain1 = jnp.sum(grad_normed * unit_first, (0, 1))
    grad_bias1 = jnp.sum(grad_normed, (0, 1))
    grad_first = norm_back(grad_normed, unit_first, inv_first, norm_values[0])
    res_low = narrow_gather(grad_first.astype(bf16))
    out_mine = lax.dynamic_slice_in_dim(wout, n_i * 192, 192, 0)
    grad_attn = jnp.einsum("fd,std->sft", out_mine, res_low, preferred_element_type=f32).astype(
        bf16
    )
    delta = jnp.sum(
        grad_attn.astype(f32).reshape(seqs, 3, HEAD, slots) * attended, 2
    )

    def three(x):
        hi = lax.reduce_precision(x, 8, 7)
        mid = lax.reduce_precision(x - hi, 8, 7)
        low = x - hi - mid
        return jnp.stack([hi, mid, low], 2).reshape(seqs, 9, slots).astype(bf16)

    grad_norm_rows = jnp.stack([grad_gain1, grad_bias1, grad_gain2, grad_bias2])
    sent_back = jnp.concatenate(
        [
            grad_attn,
            three(-lse),
            grad_norm_rows.reshape(seqs, 6, slots).astype(bf16),
            jnp.zeros((seqs, 1, slots), bf16),
            three(-delta),
            jnp.zeros((seqs, 7, slots), bf16),
        ],
        axis=1,
    )
    g_all = gather(sent_back, QAX, NQ)

    grads_packed = jnp.concatenate(
        [
            grad_wgate.astype(bf16).reshape(32, 24, width),
            grad_wup.astype(bf16).reshape(32, 24, width),
            grad_wdown.astype(bf16)
            .reshape(8, 4, 24, width)
            .transpose(1, 0, 2, 3)
            .reshape(32, 24, width),
        ],
        axis=1,
    )
    grads_packed, g_all = lax.optimization_barrier((grads_packed, g_all))
    grads_got = exchange(grads_packed, WIDE)
    dq_parts, *dkv_parts = attend_back(lengths, place, q_all, kv_all, g_all)
    grads_got, dq_parts, dkv_parts = lax.optimization_barrier((grads_got, dq_parts, dkv_parts))
    grads_got = jnp.sum(grads_got.astype(f32), 0)
    sum_gate = grads_got[0:24]
    sum_up = grads_got[24:48]
    down_rows = lax.ppermute(grads_got[48:72].astype(bf16), ("y",) + NARROW, turn_pairs)

    dkv_got = [dkv_parts[0]] + [along(dkv_parts[back], "y", NK - back) for back in range(1, NK)]
    res_cols = jnp.pad(
        lax.dynamic_slice_in_dim(res_low, n_i * 192, 192, 2), ((0, 0), (0, 0), (576, 0))
    )
    grad_proj, grad_last, norm_sums = last(
        exchange(dq_parts, QAX), dkv_got, cosine, sine, tokens, attn_all, res_cols
    )
    norm_sums = norm_sums[:, :6].reshape(4, 32, 24)
    norm_sums = lax.dynamic_index_in_dim(norm_sums, wide_i, 1, keepdims=False)
    input_part = jnp.einsum("sft,df->std", grad_proj, wqkv, preferred_element_type=f32)
    grad_input = (grad_first + sum_to_own(input_part)).astype(bf16)
    last_got = jnp.sum(exchange(grad_last.reshape(32, 24, width), WIDE).astype(f32), 0)
    sum_out = last_got[:, 576:]
    back_sent = jnp.stack(
        [
            sum(
                jnp.where(sources[k] == to, last_got[:, 192 * k : 192 * k + 192], 0.0)
                for k in range(3)
            )
            for to in range(4)
        ]
    ).astype(bf16)
    norm_sent = jnp.pad(norm_sums[:, None, :], ((0, 0), (0, 7), (0, 168))).astype(bf16)
    down_sent = down_rows.reshape(24, 4, 192).transpose(1, 0, 2)
    back_got = exchange(jnp.concatenate([back_sent, down_sent, norm_sent], 1), NARROW).astype(f32)
    sum_down = back_got[:, 24:48].reshape(96, 192)
    sum_norms = jnp.sum(back_got[:, 48, :24], 0)[None]
    sum_qkv = jnp.concatenate(
        [entry(back_got[:, :24], (3 * n_i + i) % 4) for i in range(3)], axis=1
    )
    return (layer_out, grad_input, sum_qkv, sum_out, sum_gate, sum_up, sum_down, sum_norms)


def solution(mesh):
    fine = Mesh(mesh.devices.reshape(4, 4, 2, 2, 2), AXES)
    token = P(None, WIDE + NARROW, None)
    weight = P(WIDE, NARROW)
    norm = P(NARROW, WIDE)
    return jax.shard_map(
        on_device,
        mesh=fine,
        in_specs=(token, P(), weight, weight, weight, weight, weight, norm, token),
        out_specs=(token, token, weight, weight, weight, weight, weight, norm),
        check_vma=False,
    )
```

```python
import functools
import math

import jax
import jax.numpy as jnp
from jax import lax
from jax.experimental import pallas as pl
from jax.experimental.pallas import tpu as pltpu
from jax.sharding import Mesh
from jax.sharding import PartitionSpec as P

HEADS = 12
HEAD = 64
EPSILON = 1e-05
AXES = ("y", "z", "xh", "xl", "c")
WIDE = ("y", "z", "xh")
NARROW = ("xl", "c")
QAX = ("z", "xh")
NQ = 8
NK = 4
STEP = 4
LOG2E = math.log2(math.e)
NEG = -1e30
f32 = jnp.float32
bf16 = jnp.bfloat16


def exchange(x, axes):
    return lax.all_to_all(x, axes, 0, 0, tiled=True)


def gather(x, axes, n):
    return exchange(jnp.broadcast_to(x[None], (n,) + x.shape), axes)


def along(x, axis, by):
    return lax.ppermute(x, axis, [(i, (i + by) % 4) for i in range(4)])


def after(x, *others):
    return lax.optimization_barrier((x,) + others)[0]


def round_x_z(rows):
    rows = rows.reshape(-1, 8, rows.shape[-1])
    arrived = flip(rows, "xh")
    rows = jnp.stack([rows, arrived])
    return [rows] + [along(rows, "z", back) for back in range(1, 4)], arrived


def round_y(rows):
    before, behind = along(rows, "y", 1), along(rows, "y", 3)
    return [rows, before, along(before[:2], "y", 1), along(behind[2:], "y", 3), behind]


def entry(x, index):
    return lax.dynamic_index_in_dim(x, index, 0, keepdims=False)


def in_order(mine, other, index):
    return jnp.stack([jnp.where(index == 0, mine, other), jnp.where(index == 0, other, mine)])


def flip(x, axis):
    return lax.ppermute(x, axis, [(0, 1), (1, 0)])


def layer_norm_parts(residual, gain_vec, bias_vec):
    row_mean = jnp.mean(residual, -1, keepdims=True)
    centred = residual - row_mean
    variance = jnp.mean(centred * centred, -1, keepdims=True)
    inv_std = lax.rsqrt(variance + EPSILON)
    unit_rows = centred * inv_std
    return (unit_rows * gain_vec + bias_vec, unit_rows, inv_std)


def norm_back(incoming, unit_rows, inv_std, gain_vec):
    scaled = incoming * gain_vec
    return inv_std * (
        scaled
        - jnp.mean(scaled, -1, keepdims=True)
        - unit_rows * jnp.mean(scaled * unit_rows, -1, keepdims=True)
    )


def sum_to_own(part):
    seqs, slots, width = part.shape
    cells = part.reshape(seqs, 2, 2, slots // 4, width)
    ci, xi = lax.axis_index("c"), lax.axis_index("xl")
    mine = lax.dynamic_index_in_dim(cells, ci, 2, keepdims=False)
    theirs = lax.dynamic_index_in_dim(cells, 1 - ci, 2, keepdims=False)
    half = mine.astype(f32) + flip(theirs.astype(bf16), "c").astype(f32)
    mine = lax.dynamic_index_in_dim(half, xi, 1, keepdims=False)
    theirs = lax.dynamic_index_in_dim(half, 1 - xi, 1, keepdims=False)
    return mine + flip(theirs.astype(bf16), "xl").astype(f32)


def narrow_gather(x):
    return lax.all_gather(x, NARROW, axis=1, tiled=True)


def split3(x):
    hi = x.astype(bf16)
    rest = x - hi.astype(f32)
    mid = rest.astype(bf16)
    low = (rest - mid.astype(f32)).astype(bf16)
    return hi, mid, low


def key_bias(lens_ref, start, seq):
    slot = start + lax.broadcasted_iota(jnp.int32, (16, 256), 1)
    row = lax.broadcasted_iota(jnp.int32, (16, 256), 0)
    bias = jnp.where(slot < lens_ref[seq], 0.0, NEG)
    return jnp.where(row == 0, bias, jnp.where(row < 4, 1.0, 0.0)).astype(bf16)


def key_places(place_ref):
    places = []
    for back in range(NK):
        row = (place_ref[0] + NK - back) % NK
        places.append((pl.ds(pl.multiple_of(256 * row, 256), 256), place_ref[1] + 2048 * row))
    return places


def pick_tiles(lens_ref, place_ref, seq, run):
    n = jnp.int32(0)
    for tile in range(NK):
        n = n + (place_ref[1] + 2048 * tile < lens_ref[seq]).astype(jnp.int32)
    for tiles in range(1, NK + 1):
        pl.when(n == tiles)(functools.partial(run, seq, tiles))


def attend_kernel(
    lens_ref, place_ref, q_ref, kv0, kv1, kv2, kv3, out_ref, kx_ref, vx_ref, sum_ref, peak_ref
):
    row = lax.broadcasted_iota(jnp.int32, (16, 256), 0)
    one_row = jnp.where(row == 0, 1.0, 0.0).astype(bf16)
    one_rows = jnp.concatenate([one_row] * STEP, 1)
    for seq in range(2):
        for kv_ref, (here, start) in zip((kv0, kv1, kv2, kv3), key_places(place_ref)):
            extra = key_bias(lens_ref, start, seq)
            for h in range(3):
                kt = jnp.concatenate([kv_ref[seq, pl.ds(64 * h, 64), :], extra], 0)
                kx_ref[seq, h, here, :] = jnp.transpose(kt)
                vx_ref[seq, h, pl.ds(0, 64), here] = kv_ref[seq, pl.ds(192 + 64 * h, 64), :]
                vx_ref[seq, h, pl.ds(64, 16), here] = one_row

    def run(seq, tiles, bounded):
        keys = pl.ds(0, 256 * tiles)

        @pl.loop(0, NQ // STEP)
        def _(turn):
            for h in range(3):
                q = [q_ref[turn * STEP + j, seq, pl.ds(64 * h, 64), :] for j in range(STEP)]
                qx = jnp.concatenate([jnp.concatenate(q, 1), one_rows], 0)
                s = jnp.dot(kx_ref[seq, h, keys, :], qx, preferred_element_type=f32)
                if bounded:
                    peak = jnp.zeros((1, 256 * STEP), f32)
                    p = jnp.exp2(s).astype(bf16)
                else:
                    peak = jnp.max(s, 0, keepdims=True)
                    p = jnp.exp2(s - peak).astype(bf16)
                o = jnp.dot(vx_ref[seq, h, :, keys], p, preferred_element_type=f32)
                total = o[64:65]
                o = (o[:64] * (1.0 / total)).astype(bf16)
                for j in range(STEP):
                    here = slice(256 * j, 256 * j + 256)
                    out_ref[turn * STEP + j, seq, pl.ds(64 * h, 64), :] = o[:, here]
                    sum_ref[turn * STEP + j, seq, pl.ds(h, 1), :] = total[:, here]
                    peak_ref[turn * STEP + j, seq, pl.ds(h, 1), :] = peak[:, here]

    top_key = jnp.zeros((1, 256), f32)
    for kv_ref in (kv0, kv1, kv2, kv3):
        for seq in range(2):
            for h in range(3):
                k = kv_ref[seq, pl.ds(64 * h, 64), :].astype(f32)
                top_key = jnp.maximum(top_key, jnp.sum(k * k, 0, keepdims=True))

    def widest(block, top):
        for seq in range(2):
            for h in range(3):
                q = q_ref[block, seq, pl.ds(64 * h, 64), :].astype(f32)
                top = jnp.maximum(top, jnp.sum(q * q, 0, keepdims=True))
        return top

    top_query = lax.fori_loop(0, NQ, widest, jnp.zeros((1, 256), f32))
    bounded = jnp.max(top_key) * jnp.max(top_query) < 100.0**2

    @pl.when(bounded)
    def _():
        for seq in range(2):
            pick_tiles(lens_ref, place_ref, seq, functools.partial(run, bounded=True))

    @pl.when(jnp.logical_not(bounded))
    def _():
        for seq in range(2):
            run(seq, NK, False)

    for seq in range(2):
        for block in range(NQ):
            lse = peak_ref[block, seq, pl.ds(0, 3), :] + jnp.log2(sum_ref[block, seq, pl.ds(0, 3), :])
            rows = [part.astype(f32) for part in split3(lse)] + [jnp.zeros((7, 256), f32)]
            out_ref[block, seq, pl.ds(192, 16), :] = jnp.concatenate(rows, 0).astype(bf16)


def attend_back_kernel(
    lens_ref, place_ref, q_ref, kv0, kv1, kv2, kv3, g_ref, dq_ref, dkv0, dkv1, dkv2, dkv3,
    kx_ref, vx_ref, kt_ref, dk_ref, dv_ref,
):
    row = lax.broadcasted_iota(jnp.int32, (16, 256), 0)
    ones = jnp.where(row < 3, 1.0, 0.0).astype(bf16)
    one = jnp.ones((1, 256), f32)
    nt = (((1,), (1,)), ((), ()))
    for seq in range(2):
        for kv_ref, (here, start) in zip((kv0, kv1, kv2, kv3), key_places(place_ref)):
            extra = key_bias(lens_ref, start, seq)
            for h in range(3):
                k = kv_ref[seq, pl.ds(64 * h, 64), :]
                v = kv_ref[seq, pl.ds(192 + 64 * h, 64), :]
                kx_ref[seq, h, here, :] = jnp.transpose(jnp.concatenate([k, extra], 0))
                vx_ref[seq, h, here, :] = jnp.transpose(jnp.concatenate([v, ones], 0))
                kt_ref[seq, h, :, here] = k
    dk_ref[...] = jnp.zeros_like(dk_ref)
    dv_ref[...] = jnp.zeros_like(dv_ref)

    def run(seq, tiles):
        keys = pl.ds(0, 256 * tiles)

        @pl.loop(0, NQ)
        def _(block):
            stats = g_ref[block, seq, pl.ds(192, 32), :].astype(f32)
            for h in range(3):
                q = q_ref[block, seq, pl.ds(64 * h, 64), :]
                g = g_ref[block, seq, pl.ds(64 * h, 64), :]
                rows = [one, stats[3 * h : 3 * h + 3], jnp.zeros((12, 256), f32)]
                qx = jnp.concatenate([q, jnp.concatenate(rows, 0).astype(bf16)], 0)
                rows = [stats[16 + 3 * h : 16 + 3 * h + 3], jnp.zeros((13, 256), f32)]
                gx = jnp.concatenate([g, jnp.concatenate(rows, 0).astype(bf16)], 0)
                p = jnp.exp2(jnp.dot(kx_ref[seq, h, keys, :], qx, preferred_element_type=f32))
                d = jnp.dot(vx_ref[seq, h, keys, :], gx, preferred_element_type=f32)
                ds = (p * d).astype(bf16)
                dq = jnp.dot(kt_ref[seq, h, :, keys], ds, preferred_element_type=f32)
                dk_ref[seq, h, :, keys] += lax.dot_general(q, ds, nt, preferred_element_type=f32)
                dv_ref[seq, h, :, keys] += lax.dot_general(
                    g, p.astype(bf16), nt, preferred_element_type=f32
                )
                dq_ref[block, seq, pl.ds(64 * h, 64), :] = (dq * HEAD**-0.5).astype(bf16)

    for seq in range(2):
        pick_tiles(lens_ref, place_ref, seq, run)
    for seq in range(2):
        extra = sum(g_ref[block, seq, pl.ds(192, 32), :].astype(f32) for block in range(NQ))
        extra = jnp.concatenate([extra[9:15], jnp.zeros((10, 256), f32)], 0).astype(bf16)
        for dkv_ref, (here, _) in zip((dkv0, dkv1, dkv2, dkv3), key_places(place_ref)):
            dkv_ref[seq, pl.ds(384, 16), :] = extra
            for h in range(3):
                dk = dk_ref[seq, h, :, here] * (1.0 / LOG2E)
                dkv_ref[seq, pl.ds(64 * h, 64), :] = dk.astype(bf16)
                dkv_ref[seq, pl.ds(192 + 64 * h, 64), :] = dv_ref[seq, h, :, here].astype(bf16)


def unpack_kernel(where_ref, *refs):
    first, second = refs[:5], refs[5:10]
    gate_ref, up_ref, out_ref, down_ref, norm_ref = refs[10:]
    for back_y in range(4):
        y = (where_ref[0] + 4 - back_y) % 4
        for back_z in range(4):
            z = (where_ref[1] + 4 - back_z) % 4
            index, inner = ((0, 1, 2, 4)[back_y], back_z)
            if back_y == 2 and back_z >= 2:
                index, inner = 3, back_z - 2
            for back_x in range(2):
                x = (where_ref[2] + back_x) % 2
                row = (y * 4 + z) * 2 + x
                block = first[index].at[inner, back_x]
                gate_ref[row] = block[0:3]
                up_ref[row] = block[3:6]
                block = second[index].at[inner, back_x]
                out_ref[row] = block[0:3]
                down_ref[(z * 2 + x) * 4 + y] = block[3:6]
                norm_ref[row] = block[6]


def last_kernel(
    dq_ref, d0, d1, d2, d3, cos_ref, sin_ref, tokens_ref, attn_ref, res_ref, proj_ref, grad_ref, norm_ref
):
    cosine, sine = cos_ref[...], sin_ref[...]
    grad = None
    for seq in range(2):
        dq = sum(dq_ref[block, seq].astype(f32) for block in range(NQ))
        dkv = sum(part[seq].astype(f32) for part in (d0, d1, d2, d3))
        norm_ref[seq] = dkv[384:392]
        rows = []
        for source in (dq, dkv):
            for h in range(3):
                first, second = source[64 * h : 64 * h + 32], source[64 * h + 32 : 64 * h + 64]
                rows += [first * cosine + second * sine, second * cosine - first * sine]
        rows.append(dkv[192:384])
        proj = jnp.concatenate(rows, 0).astype(bf16)
        proj_ref[seq] = proj
        wide = jnp.concatenate([proj, jnp.zeros((192, 256), bf16)], 0)
        part = lax.dot_general(
            jnp.transpose(tokens_ref[seq]), wide, (((1,), (1,)), ((), ())),
            preferred_element_type=f32,
        ) + jnp.dot(attn_ref[seq], res_ref[seq], preferred_element_type=f32)
        grad = part if grad is None else grad + part
    grad_ref[...] = grad.astype(bf16)


SMEM = pl.BlockSpec(memory_space=pltpu.SMEM)
VMEM = pl.BlockSpec(memory_space=pltpu.VMEM)
PARAMS = pltpu.CompilerParams(vmem_limit_bytes=56 * 1024 * 1024)


def attend(lengths, place, q_all, kv_all):
    return pl.pallas_call(
        attend_kernel,
        out_shape=jax.ShapeDtypeStruct((NQ, 2, 208, 256), bf16),
        in_specs=[SMEM, SMEM] + [VMEM] * 5,
        out_specs=VMEM,
        scratch_shapes=[
            pltpu.VMEM((2, 3, 1024, 80), bf16),
            pltpu.VMEM((2, 3, 80, 1024), bf16),
            pltpu.VMEM((NQ, 2, 8, 256), f32),
            pltpu.VMEM((NQ, 2, 8, 256), f32),
        ],
        compiler_params=PARAMS,
        cost_estimate=pl.CostEstimate(
            flops=23_000_000_000, bytes_accessed=5_000_000, transcendentals=12_582_912
        ),
    )(lengths, place, q_all, *kv_all)


def attend_back(lengths, place, q_all, kv_all, g_all):
    return pl.pallas_call(
        attend_back_kernel,
        out_shape=(
            jax.ShapeDtypeStruct((NQ, 2, 192, 256), bf16),
        )
        + (jax.ShapeDtypeStruct((2, 400, 256), bf16),) * NK,
        in_specs=[SMEM, SMEM] + [VMEM] * 6,
        out_specs=(VMEM,) * 5,
        scratch_shapes=[
            pltpu.VMEM((2, 3, 1024, 80), bf16),
            pltpu.VMEM((2, 3, 1024, 80), bf16),
            pltpu.VMEM((2, 3, 64, 1024), bf16),
            pltpu.VMEM((2, 3, 64, 1024), f32),
            pltpu.VMEM((2, 3, 64, 1024), f32),
        ],
        compiler_params=PARAMS,
        cost_estimate=pl.CostEstimate(
            flops=46_000_000_000, bytes_accessed=8_000_000, transcendentals=12_582_912
        ),
    )(lengths, place, q_all, *kv_all, g_all)


def unpack(where, parts):
    block = jax.ShapeDtypeStruct((32, 3, 8, 768), bf16)
    *weights, norms = pl.pallas_call(
        unpack_kernel,
        out_shape=(block,) * 4 + (jax.ShapeDtypeStruct((32, 8, 768), bf16),),
        in_specs=[SMEM] + [VMEM] * 10,
        out_specs=(VMEM,) * 5,
        compiler_params=PARAMS,
        cost_estimate=pl.CostEstimate(flops=0, bytes_accessed=12_000_000, transcendentals=0),
    )(where, *parts)
    return [weight.reshape(768, 768) for weight in weights], norms


def last(dq, dkv, cosine, sine, tokens, attn, res):
    return pl.pallas_call(
        last_kernel,
        out_shape=(
            jax.ShapeDtypeStruct((2, 576, 256), bf16),
            jax.ShapeDtypeStruct((768, 768), bf16),
            jax.ShapeDtypeStruct((2, 8, 256), f32),
        ),
        in_specs=[VMEM] * 10,
        out_specs=(VMEM,) * 3,
        compiler_params=PARAMS,
        cost_estimate=pl.CostEstimate(
            flops=1_300_000_000, bytes_accessed=8_000_000, transcendentals=0
        ),
    )(dq, *dkv, cosine, sine, tokens, attn, res)


def on_device(hidden_in, lengths, w_qkv, w_out, w_gate, w_up, w_down, norm_params, cotangent):
    y_i, z_i, xh_i = (lax.axis_index(a) for a in WIDE)
    wide_i = (y_i * 4 + z_i) * 2 + xh_i
    n_i = lax.axis_index("xl") * 2 + lax.axis_index("c")
    seqs, own_slots, width = hidden_in.shape
    slots = own_slots * 4

    first_z, _ = round_x_z(jnp.concatenate([w_gate, w_up]))
    sent = []
    for to in range(4):
        pick = (to - 3 * n_i) % 4
        block = jnp.where(
            pick == 0, w_qkv[:, :192], jnp.where(pick == 1, w_qkv[:, 192:384], w_qkv[:, 384:])
        )
        norm_row = jnp.pad(norm_params, ((0, 7), (0, 168)))
        sent.append(jnp.concatenate([block, w_out, w_down[24 * to : 24 * to + 24], norm_row]))
    sent = jnp.stack(sent)
    got = exchange(sent, NARROW)
    sources = [(4 * k + n_i) // 3 for k in range(3)]
    qkv_mine = jnp.concatenate([entry(got[:, :24], source) for source in sources], axis=1)
    wqkv = gather(qkv_mine, WIDE, 32).reshape(width, 576)

    pair = in_order(hidden_in, flip(after(hidden_in, sent), "xl"), lax.axis_index("xl"))
    tokens = in_order(pair, flip(pair, "c"), lax.axis_index("c"))
    tokens = tokens.transpose(2, 1, 0, 3, 4).reshape(seqs, slots, width)

    turn_pairs = [((y * 4 + n), (n * 4 + y)) for y in range(4) for n in range(4)]
    down_rows = got[:, 48:72].transpose(1, 0, 2).reshape(24, width)
    down_rows = lax.ppermute(down_rows, ("y",) + NARROW, turn_pairs)
    out_rows = got[:, 24:48].transpose(1, 0, 2).reshape(24, width)
    norm_row = jnp.pad(got[:, 72, :24].reshape(1, 96), ((0, 7), (0, width - 96)))
    second_z, second_x = round_x_z(jnp.concatenate([out_rows, down_rows, norm_row]))
    first_rows = jnp.stack(first_z)
    first_parts = round_y(first_rows)
    place = jnp.stack([y_i, (z_i * 2 + xh_i) * slots]).astype(jnp.int32)
    wqkv = after(wqkv, *first_z[1:], second_x, place)

    positions = wide_i * slots + jnp.arange(slots)
    freqs = 10000.0 ** (-2.0 * jnp.arange(HEAD // 2, dtype=f32) / HEAD)
    angles = freqs[:, None] * positions.astype(f32)[None, :]
    cosine, sine = jnp.cos(angles), jnp.sin(angles)
    projected = jnp.einsum("df,std->sft", wqkv, tokens, preferred_element_type=f32)

    def rotate(block):
        halves = block.reshape(seqs, 3, 2, HEAD // 2, slots)
        first, second = halves[:, :, 0], halves[:, :, 1]
        return jnp.stack(
            [first * cosine - second * sine, second * cosine + first * sine], 2
        ).reshape(seqs, 192, slots)

    query = (rotate(projected[:, :192]) * (HEAD**-0.5 * LOG2E)).astype(bf16)
    keyval = jnp.concatenate(
        [rotate(projected[:, 192:384]), projected[:, 384:]], axis=1
    ).astype(bf16)
    q_all = gather(query, QAX, NQ)
    kv_all = [keyval] + [along(keyval, "y", back) for back in range(1, NK)]
    second_parts = round_y(jnp.stack(after(second_z, kv_all[1])))
    place = after(place, first_parts[1], first_parts[4])
    parts = attend(lengths, place, q_all, kv_all)
    parts = after(parts, *first_parts, second_parts[1], second_parts[4])
    parts = exchange(parts, QAX).astype(f32)
    part_lse = jnp.sum(parts[:, :, 192:201].reshape(NQ, seqs, 3, 3, slots), 2)
    top = jnp.max(part_lse, 0)
    lse = top + jnp.log2(jnp.sum(jnp.exp2(part_lse - top), 0))
    shares = jnp.exp2(part_lse - lse)
    where = jnp.stack([y_i, z_i, xh_i]).astype(jnp.int32)
    (wgate, wup, wout, wdown), norms = unpack(where, first_parts + second_parts)
    norm_values = (
        norms[:, 0, :96].reshape(32, 4, 24).transpose(1, 0, 2).reshape(4, width).astype(f32)
    )
    attended = jnp.sum(
        parts[:, :, :192].reshape(NQ, seqs, 3, HEAD, slots) * shares[:, :, :, None, :], 0
    )
    attn_sent = attended.reshape(seqs, 192, slots).astype(bf16)
    attn_all = narrow_gather(attn_sent)

    projection = jnp.einsum("sft,fd->std", attn_all, wout, preferred_element_type=f32)
    normed, _, _ = layer_norm_parts(
        tokens.astype(f32) + projection, norm_values[0], norm_values[1]
    )
    normed_low = normed.astype(bf16)
    own_slice = lambda a: lax.dynamic_slice_in_dim(a, n_i * own_slots, own_slots, 1)
    own_first, unit_first, inv_first = layer_norm_parts(
        hidden_in.astype(f32) + own_slice(projection), norm_values[0], norm_values[1]
    )
    flat_low = normed_low.reshape(-1, width)
    gate_pre = jnp.dot(flat_low, wgate, preferred_element_type=f32)
    up_pre = jnp.dot(flat_low, wup, preferred_element_type=f32)
    gate_sigmoid = jax.nn.sigmoid(gate_pre)
    gate_silu = gate_pre * gate_sigmoid
    activated = (gate_silu * up_pre).astype(bf16)
    down_part = jnp.dot(activated, wdown, preferred_element_type=f32)
    down_out = sum_to_own(down_part.reshape(seqs, slots, width))
    output_rows, unit_second, inv_second = layer_norm_parts(
        own_first + down_out, norm_values[2], norm_values[3]
    )
    own_positions = wide_i * slots + n_i * own_slots + jnp.arange(own_slots)
    valid = (own_positions[None, :] < lengths[:, None]).astype(f32)[:, :, None]
    layer_out = (output_rows * valid).astype(bf16)
    grad_rows = cotangent.astype(f32) * valid
    grad_gain2 = jnp.sum(grad_rows * unit_second, (0, 1))
    grad_bias2 = jnp.sum(grad_rows, (0, 1))
    grad_second = norm_back(grad_rows, unit_second, inv_second, norm_values[2])
    down_low = narrow_gather(grad_second.astype(bf16)).reshape(-1, width)

    grad_wdown = jnp.einsum("tf,td->fd", activated, down_low, preferred_element_type=f32)
    grad_act = jnp.einsum("td,fd->tf", down_low, wdown, preferred_element_type=f32)
    silu_slope = gate_sigmoid * (1.0 + gate_pre * (1.0 - gate_sigmoid))
    grad_gate_low = (grad_act * up_pre * silu_slope).astype(bf16)
    grad_up_low = (grad_act * gate_silu).astype(bf16)
    grad_wgate = jnp.einsum("td,tf->df", flat_low, grad_gate_low, preferred_element_type=f32)
    grad_wup = jnp.einsum("td,tf->df", flat_low, grad_up_low, preferred_element_type=f32)
    first_part = jnp.einsum(
        "tf,df->td", grad_gate_low, wgate, preferred_element_type=f32
    ) + jnp.einsum("tf,df->td", grad_up_low, wup, preferred_element_type=f32)
    grad_normed = grad_second + sum_to_own(first_part.reshape(seqs, slots, width))
    grad_gain1 = jnp.sum(grad_normed * unit_first, (0, 1))
    grad_bias1 = jnp.sum(grad_normed, (0, 1))
    grad_first = norm_back(grad_normed, unit_first, inv_first, norm_values[0])
    res_low = narrow_gather(grad_first.astype(bf16))
    out_mine = lax.dynamic_slice_in_dim(wout, n_i * 192, 192, 0)
    grad_attn = jnp.einsum("fd,std->sft", out_mine, res_low, preferred_element_type=f32).astype(
        bf16
    )
    delta = jnp.sum(
        grad_attn.astype(f32).reshape(seqs, 3, HEAD, slots) * attended, 2
    )

    def three(x):
        hi = lax.reduce_precision(x, 8, 7)
        mid = lax.reduce_precision(x - hi, 8, 7)
        low = x - hi - mid
        return jnp.stack([hi, mid, low], 2).reshape(seqs, 9, slots).astype(bf16)

    grad_norm_rows = jnp.stack([grad_gain1, grad_bias1, grad_gain2, grad_bias2])
    sent_back = jnp.concatenate(
        [
            grad_attn,
            three(-lse),
            grad_norm_rows.reshape(seqs, 6, slots).astype(bf16),
            jnp.zeros((seqs, 1, slots), bf16),
            three(-delta),
            jnp.zeros((seqs, 7, slots), bf16),
        ],
        axis=1,
    )
    g_all = gather(sent_back, QAX, NQ)

    grads_packed = jnp.concatenate(
        [
            grad_wgate.astype(bf16).reshape(32, 24, width),
            grad_wup.astype(bf16).reshape(32, 24, width),
            grad_wdown.astype(bf16)
            .reshape(8, 4, 24, width)
            .transpose(1, 0, 2, 3)
            .reshape(32, 24, width),
        ],
        axis=1,
    )
    grads_packed, g_all = lax.optimization_barrier((grads_packed, g_all))
    grads_got = exchange(grads_packed, WIDE)
    dq_parts, *dkv_parts = attend_back(lengths, place, q_all, kv_all, g_all)
    grads_got, dq_parts, dkv_parts = lax.optimization_barrier((grads_got, dq_parts, dkv_parts))
    grads_got = jnp.sum(grads_got.astype(f32), 0)
    sum_gate = grads_got[0:24]
    sum_up = grads_got[24:48]
    down_rows = lax.ppermute(grads_got[48:72].astype(bf16), ("y",) + NARROW, turn_pairs)

    dkv_got = [dkv_parts[0]] + [along(dkv_parts[back], "y", NK - back) for back in range(1, NK)]
    res_cols = jnp.pad(
        lax.dynamic_slice_in_dim(res_low, n_i * 192, 192, 2), ((0, 0), (0, 0), (576, 0))
    )
    grad_proj, grad_last, norm_sums = last(
        exchange(dq_parts, QAX), dkv_got, cosine, sine, tokens, attn_all, res_cols
    )
    norm_sums = norm_sums[:, :6].reshape(4, 32, 24)
    norm_sums = lax.dynamic_index_in_dim(norm_sums, wide_i, 1, keepdims=False)
    input_part = jnp.einsum("sft,df->std", grad_proj, wqkv, preferred_element_type=f32)
    grad_input = (grad_first + sum_to_own(input_part)).astype(bf16)
    last_got = jnp.sum(exchange(grad_last.reshape(32, 24, width), WIDE).astype(f32), 0)
    sum_out = last_got[:, 576:]
    back_sent = jnp.stack(
        [
            sum(
                jnp.where(sources[k] == to, last_got[:, 192 * k : 192 * k + 192], 0.0)
                for k in range(3)
            )
            for to in range(4)
        ]
    ).astype(bf16)
    norm_sent = jnp.pad(norm_sums[:, None, :], ((0, 0), (0, 7), (0, 168))).astype(bf16)
    down_sent = down_rows.reshape(24, 4, 192).transpose(1, 0, 2)
    back_got = exchange(jnp.concatenate([back_sent, down_sent, norm_sent], 1), NARROW).astype(f32)
    sum_down = back_got[:, 24:48].reshape(96, 192)
    sum_norms = jnp.sum(back_got[:, 48, :24], 0)[None]
    sum_qkv = jnp.concatenate(
        [entry(back_got[:, :24], (3 * n_i + i) % 4) for i in range(3)], axis=1
    )
    return (layer_out, grad_input, sum_qkv, sum_out, sum_gate, sum_up, sum_down, sum_norms)


def solution(mesh):
    fine = Mesh(mesh.devices.reshape(4, 4, 2, 2, 2), AXES)
    token = P(None, WIDE + NARROW, None)
    weight = P(WIDE, NARROW)
    norm = P(NARROW, WIDE)
    return jax.shard_map(
        on_device,
        mesh=fine,
        in_specs=(token, P(), weight, weight, weight, weight, weight, norm, token),
        out_specs=(token, token, weight, weight, weight, weight, weight, norm),
        check_vma=False,
    )
```
